32 devices in a mesh: shots: 2 (over x), depth: 16 (over z, y, core).
Axes of the slice: x: 2, y: 2, z: 4, core: 2. Of those that a mesh axis runs over, the one named last changes fastest.
Arguments:
- fields_in: float32 [16, 4, 64, 2048], P('depth', None, 'shots'), parts along dimension 2, may hold values from -6 to 6
- flight_angular: float32 [16, 64], P('depth', 'shots'), parts along dimension 1, may hold values from 0.6 to 3
- wavelet: float32 [3, 2, 64], P(None, None, 'shots'), parts along dimension 2, may hold values from -6 to 6
- surface_angular: float32 [3, 64], P(None, 'shots'), parts along dimension 1, may hold values from 0.6 to 3
- records: float32 [3, 2, 64, 1024], P(None, None, 'shots'), parts along dimension 2, may hold values from -6 to 6
- source_pos: int32 [2], P('shots'), parts along dimension 0, may hold values from 0 to 2047
- receiver_pos: int32 [2048], P('shots'), parts along dimension 0, may hold values from 0 to 2047
- vel_table: float32 [64, 16], P('depth'), may hold values from 1.5 to 4.5
- vel_index: int32 [64, 2048], P('depth'), may hold values from 0 to 15
Outputs:
- section: float32 [64, 4096], P('depth', 'shots'), parts along dimension 1
- fields_out: float32 [16, 4, 64, 2048], P('depth', None, 'shots'), parts along dimension 2
The draws below stay inside these ranges and needn't reach their ends.
There are 2 independent parts, one for each index of `shots`. The reference program is written for one: setup_inputs(seed, part) draws one part's arguments, and reference() takes and returns one part's arrays. A program takes and returns all parts, laid end to end along the dimension named above; an argument that names none is the same for every part. Nothing has to cross between parts.
All inputs are finite; a program needn't handle non-finite values.
Results may differ from the reference program's by a relative error of at most 0.0003.
Values sent between devices are 32-bit elements; how exact they have to be, the bound alone decides.
No kernel may reach another device: no remote copies, remote signals or barrier semaphores. Data moves between devices by JAX's collectives and lax.ppermute only.
A program may use at most 64 MiB of HBM per device.

```python
import math
import jax
import jax.numpy as jnp
from jax import lax

NX = 2048
FB = 32
NREC = 1024
LAYERS = 4
TICKS = 3
NV = 16
NZ = 64
N_DEPTH = 16


def plant(values, key, low, largest):
    index_at = [jax.random.randint(jax.random.fold_in(key, axis), (), 0, length) for axis, length in enumerate(values.shape)]
    main_axis = values.shape.index(max(values.shape))
    beside = index_at[:main_axis] + [(index_at[main_axis] + 1) % values.shape[main_axis]] + index_at[main_axis + 1:]
    return values.at[tuple(index_at)].set(low).at[tuple(beside)].set(largest)


def level_of(key, shape, shards, smallest, largest):
    loudness, own = 1.0, jax.random.fold_in(key, 6)
    for position, shards_of in shards:
        steps = jnp.exp(jax.random.uniform(jax.random.fold_in(own, position), (shards_of,), jnp.float32, smallest / len(shards), largest / len(shards)))
        loudness = loudness * jnp.repeat(steps, shape[position] // shards_of).reshape([-1 if axis == position else 1 for axis in range(len(shape))])
    return loudness


def scatter_about(own_key, dims, deviation, most, split=(), kind=jnp.bfloat16):
    gain = level_of(own_key, dims, split, -0.22, 0.18) if split else 1.0
    values = jax.random.normal(own_key, dims, jnp.float32) * deviation * gain
    return jnp.minimum(jnp.maximum(values, -most), most).astype(kind)


def setup_inputs(seed: int = 0, part: int = 0) -> dict:
    seeds = jax.random.split(jax.random.key(seed), 10)
    part_keys = jax.random.split(jax.random.fold_in(seeds[9], part), 10)
    fields_in = scatter_about(part_keys[0], (N_DEPTH, 4, FB, NX), 1.0, 6.0, ((0, 16),), jnp.float32)
    flight_angular = jnp.clip(0.6 + 2.4 * jax.random.uniform(part_keys[1], (N_DEPTH, FB), jnp.float32) ** level_of(part_keys[1], (N_DEPTH, FB), ((0, 16),), -0.2, 0.2), 0.6, 3.0)
    wavelet = scatter_about(part_keys[2], (TICKS, 2, FB), 1.0, 6.0, (), jnp.float32)
    surface_angular = jnp.clip(jax.random.uniform(part_keys[3], (TICKS, FB), jnp.float32, 0.6, 3.0), 0.6, 3.0)
    records = scatter_about(part_keys[4], (TICKS, 2, FB, NREC), 1.0, 6.0, (), jnp.float32)
    source_pos = jax.random.randint(part_keys[5], (1,), 0, NX).astype(jnp.int32)
    receiver_pos = plant(jax.random.randint(part_keys[6], (NREC,), 0, NX), jax.random.fold_in(part_keys[6], 1), 0, NX - 1).astype(jnp.int32)
    vel_table = jnp.clip(jnp.exp(math.log(4.5) - 1.0986123 * jax.random.uniform(seeds[7], (NZ, NV), jnp.float32) ** level_of(seeds[7], (NZ, NV), ((0, 16),), -0.2, 0.2)), 1.5, 4.5)
    vel_index = plant(jax.random.randint(seeds[8], (NZ, NX), 0, NV), jax.random.fold_in(seeds[8], 1), 0, NV - 1).astype(jnp.int32)
    return dict(fields_in=fields_in, flight_angular=flight_angular, wavelet=wavelet, surface_angular=surface_angular, records=records, source_pos=source_pos, receiver_pos=receiver_pos, vel_table=vel_table, vel_index=vel_index)


depth_step = 1.0
lateral_scale = 0.03
damping = 0.3

def lateral(values):
    padded = jnp.pad(values, [(0, 0)] * (values.ndim - 1) + [(2, 2)])
    return (16.0 * (padded[..., 1:-3] + padded[..., 3:-1]) - (padded[..., :-4] + padded[..., 4:]) - 30.0 * padded[..., 2:-2]) / 12.0

def layer_step(fields, angular, velocity):
    freq_col = angular[..., :, None]
    speed_row = velocity[..., None, :]
    phase_angle = freq_col * (depth_step / speed_row)
    cosine = jnp.cos(phase_angle)
    sine_part = jnp.sin(phase_angle)
    lateral_gain = lateral_scale * speed_row / (2.0 * freq_col)
    source_real = fields[..., 0, :, :]
    source_imag = fields[..., 1, :, :]
    receiver_real = fields[..., 2, :, :]
    receiver_imag = fields[..., 3, :, :]
    rotated = jnp.stack([source_real * cosine - source_imag * sine_part, source_real * sine_part + source_imag * cosine, receiver_real * cosine + receiver_imag * sine_part, receiver_imag * cosine - receiver_real * sine_part], axis=-3)
    spread = lateral(rotated)
    new_source_real = rotated[..., 0, :, :] + lateral_gain * (damping * spread[..., 0, :, :] - spread[..., 1, :, :])
    new_source_imag = rotated[..., 1, :, :] + lateral_gain * (damping * spread[..., 1, :, :] + spread[..., 0, :, :])
    new_receiver_real = rotated[..., 2, :, :] + lateral_gain * (damping * spread[..., 2, :, :] + spread[..., 3, :, :])
    new_receiver_imag = rotated[..., 3, :, :] + lateral_gain * (damping * spread[..., 3, :, :] - spread[..., 2, :, :])
    contrib = lax.optimization_barrier(jnp.sum(new_source_real * new_receiver_real + new_source_imag * new_receiver_imag, axis=-2)) * (1.0 / math.sqrt(FB))
    result = jnp.stack([new_source_real, new_source_imag, new_receiver_real, new_receiver_imag], axis=-3)
    return (result, contrib)

def surface_block(period, wavelet, surface_angular, records, source_pos, receiver_pos, width):
    lateral_cells = jnp.arange(width, dtype=jnp.int32)
    source_spot = (lateral_cells == source_pos[0]).astype(jnp.float32)
    source_field = wavelet[period][:, :, None] * source_spot
    receiver_field = jnp.zeros((2, wavelet.shape[2], width), jnp.float32).at[:, :, receiver_pos].add(records[period])
    return (jnp.concatenate([source_field, receiver_field], 0), surface_angular[period])

def reference(fields_in, flight_angular, wavelet, surface_angular, records, source_pos, receiver_pos, vel_table, vel_index):
    chain = fields_in.shape[0]
    width = fields_in.shape[3]
    velocity = jnp.take_along_axis(vel_table, vel_index, axis=1).reshape(chain, LAYERS, width)
    fields = fields_in
    angular = flight_angular
    section = jnp.zeros((chain, LAYERS, width), jnp.float32)
    for period in range(TICKS):
        layer_rows = []
        for stratum in range(LAYERS):
            fields, contrib = layer_step(fields, angular, velocity[:, stratum])
            layer_rows.append(contrib)
        section = section + jnp.stack(layer_rows, 1)
        top_fields, top_angular = surface_block(period, wavelet, surface_angular, records, source_pos, receiver_pos, width)
        fields = jnp.concatenate([top_fields[None], fields[:-1]], 0)
        angular = jnp.concatenate([top_angular[None], angular[:-1]], 0)
    stacked = section.reshape(chain * LAYERS, width)
    padded = jnp.pad(stacked, ((1, 1), (0, 0)))
    filtered = 2.0 * stacked - 0.5 * (padded[:-2] + padded[2:])
    return (filtered, fields)
```

```python
import math

import jax
import jax.numpy as jnp
from jax import lax
from jax.experimental import pallas as pl
from jax.experimental.pallas import tpu as pltpu
from jax.sharding import PartitionSpec as P

TICKS = 3
SUB = 8
LANES = 128

depth_step = 1.0
lateral_scale = 0.03
damping = 0.3


def as_column(row):
    n = row.shape[1]
    shape = (n, n)
    same = lax.broadcasted_iota(jnp.int32, shape, 0) == lax.broadcasted_iota(jnp.int32, shape, 1)
    return jnp.sum(jnp.where(same, row, 0.0), axis=1, keepdims=True)


def three_pieces(value):
    high = value.astype(jnp.bfloat16)
    rest = value - high.astype(jnp.float32)
    mid = rest.astype(jnp.bfloat16)
    low = (rest - mid.astype(jnp.float32)).astype(jnp.bfloat16)
    return high, mid, low


def layer_tables(w_col, model, row, rows, width, levels):
    index = model[pl.ds(row, 1), :]
    speed = model[pl.ds(row + 4, 1), :][:, : 3 * levels]
    phase = w_col * (depth_step / speed)
    gain = (lateral_scale / 24.0) * speed / w_col
    table = jnp.concatenate([jnp.cos(phase), jnp.sin(phase), gain], axis=0)
    high, mid, low = three_pieces(table)
    lane = lax.broadcasted_iota(jnp.int32, table.shape, 1)
    pieces = jnp.where(
        lane < levels,
        high.astype(jnp.float32),
        jnp.where(lane < 2 * levels, mid.astype(jnp.float32), low.astype(jnp.float32)),
    ).astype(jnp.bfloat16)
    level = lax.broadcasted_iota(jnp.int32, (3 * levels, width), 0) % levels
    hot = jnp.where(level == index.astype(jnp.int32), 1.0, 0.0).astype(jnp.bfloat16)
    return jnp.dot(pieces, hot, preferred_element_type=jnp.float32)


def layer_tile(state, tables, r0, rows, emit):
    width = state.shape[2]
    blocks = width // LANES
    lane = lax.broadcasted_iota(jnp.int32, (SUB, LANES), 1)
    first, first2 = lane == 0, lane < 2
    last, last2 = lane == LANES - 1, lane >= LANES - 2
    zero = jnp.zeros((SUB, LANES), jnp.float32)
    cell, p1, p2, m1, m2, gains = {}, {}, {}, {}, {}, {}
    for j in (-1, blocks):
        p1[j] = p2[j] = m1[j] = m2[j] = [zero] * 4
    for j in range(blocks + 1):
        if j < blocks:
            at = pl.ds(j * LANES, LANES)
            sr, si, rr, ri = (state[c, pl.ds(r0, SUB), at] for c in range(4))
            cosine = tables[pl.ds(r0, SUB), at]
            sine = tables[pl.ds(rows + r0, SUB), at]
            gains[j] = tables[pl.ds(2 * rows + r0, SUB), at]
            cell[j] = [
                sr * cosine - si * sine,
                sr * sine + si * cosine,
                rr * cosine + ri * sine,
                ri * cosine - rr * sine,
            ]
            p1[j] = [pltpu.roll(v, 1, 1) for v in cell[j]]
            p2[j] = [pltpu.roll(v, 2, 1) for v in cell[j]]
            m1[j] = [pltpu.roll(v, LANES - 1, 1) for v in cell[j]]
            m2[j] = [pltpu.roll(v, LANES - 2, 1) for v in cell[j]]
        if j >= 1:
            k = j - 1
            spread = []
            for c in range(4):
                near = jnp.where(first, p1[k - 1][c], p1[k][c]) + jnp.where(last, m1[k + 1][c], m1[k][c])
                far = jnp.where(first2, p2[k - 1][c], p2[k][c]) + jnp.where(last2, m2[k + 1][c], m2[k][c])
                spread.append(16.0 * near - far - 30.0 * cell[k][c])
            g = gains[k]
            new = [
                cell[k][0] + g * (damping * spread[0] - spread[1]),
                cell[k][1] + g * (damping * spread[1] + spread[0]),
                cell[k][2] + g * (damping * spread[2] + spread[3]),
                cell[k][3] + g * (damping * spread[3] - spread[2]),
            ]
            at = pl.ds(k * LANES, LANES)
            for c in range(4):
                state[c, pl.ds(r0, SUB), at] = new[c]
            if emit is not None:
                emit(k, new[0] * new[2] + new[1] * new[3])


def surface_rows(t, f0, rows, wavelet, records, source_pos, receiver_pos, state, hits):
    width = state.shape[2]
    receivers = records.shape[3]
    hits[...] = jnp.where(
        lax.broadcasted_iota(jnp.int32, (width, receivers), 0) == receiver_pos[...], 1.0, 0.0
    ).astype(jnp.bfloat16)
    cells = lax.broadcasted_iota(jnp.int32, (rows, width), 1)
    spot = cells == source_pos[0]
    for c in range(2):
        strength = as_column(wavelet[t, pl.ds(c, 1), :])[f0 : f0 + rows]
        state[c] = jnp.where(spot, strength, 0.0)
        pieces = jnp.concatenate(three_pieces(records[t, c, f0 : f0 + rows, :]), axis=0)
        for x in range(0, width, 512):
            found = lax.dot_general(
                pieces,
                hits[x : x + 512, :],
                (((1,), (1,)), ((), ())),
                preferred_element_type=jnp.float32,
            )
            state[2 + c, :, x : x + 512] = found[:rows] + found[rows : 2 * rows] + found[2 * rows :]


def main_kernel(
    chunk, rows, devices, last_chunk,
    fields, angular, surface_angular, wavelet, records, source_pos, receiver_pos,
    model0, model1, model2, *rest,
):
    if last_chunk:
        earlier, sent, own, next1, next2, above, state, tables, totals, models, hits = rest
    else:
        sent, partial, state, tables, totals, models, hits = rest
    width = state.shape[2]
    f0 = chunk * rows
    d = lax.axis_index("depth")
    levels = 16
    for t, model in enumerate((model0, model1, model2)):
        models[8 * t : 8 * t + 8, :] = model[...]
    for c in range(4):
        state[c] = fields[0, c]
    w_own = as_column(angular[...])[f0 : f0 + rows]
    w_top = as_column(surface_angular[pl.ds(0, 1), :])[f0 : f0 + rows]

    def step(l, carry):
        @pl.when(jnp.logical_and(l == 4, d == devices - 1))
        def _():
            surface_rows(0, f0, rows, wavelet, records, source_pos, receiver_pos, state, hits)

        swapped = jnp.logical_and(l >= 4, d == devices - 1)
        w_col = jnp.where(swapped, w_top, w_own)
        row = 8 * (l // 4) + l % 4
        tables[...] = layer_tables(w_col, models, row, rows, width, levels)
        for r0 in range(0, rows, SUB):
            def emit(k, value):
                at = pl.ds(k * LANES, LANES)
                if r0 == 0:
                    totals[l, :, at] = value
                else:
                    totals[l, :, at] += value
            layer_tile(state, tables, r0, rows, emit)
        return carry

    lax.fori_loop(0, 4 * TICKS, step, 0)
    for c in range(4):
        sent[c * rows : (c + 1) * rows, :] = state[c]
    found = [jnp.sum(totals[l], axis=0, keepdims=True) for l in range(4 * TICKS)]
    if not last_chunk:
        for l in range(4 * TICKS):
            partial[l : l + 1, :] = found[l]
        return
    scale = 1.0 / math.sqrt(angular.shape[1])
    image = []
    for l in range(4 * TICKS):
        value = (found[l] + earlier[l : l + 1, :]) * scale
        if l >= 8:
            value = jnp.where(d == devices - 2, 0.0, value)
        image.append(value)
    apart = d == devices - 1

    def filtered(l):
        total = 0.0
        if 0 <= l < 4 * TICKS:
            total = 2.0 * image[l]
        if 0 <= l - 1:
            before = image[l - 1]
            total = total - 0.5 * (jnp.where(apart, 0.0, before) if l == 4 else before)
        if l + 1 < 4 * TICKS:
            after = image[l + 1]
            total = total - 0.5 * (jnp.where(apart, 0.0, after) if l == 3 else after)
        return total

    above[...] = filtered(-1)
    for l in range(4):
        own[l : l + 1, :] = filtered(l)
        next1[l : l + 1, :] = filtered(l + 4)
        next2[l : l + 1, :] = filtered(l + 8)
    sent[4 * rows : 4 * rows + 1, :] = filtered(12)


def top_kernel(
    above, surface_angular, wavelet, records, source_pos, receiver_pos, model,
    sent, extra, out, state, tables, totals, hits,
):
    width = state.shape[2]
    rows = state.shape[1]
    d = lax.axis_index("depth")
    sent[...] = jnp.zeros(sent.shape, jnp.float32)
    sent[3:4, :] = above[...]
    extra[...] = jnp.zeros(extra.shape, jnp.float32)

    @pl.when(d == 0)
    def _():
        surface_rows(2, 0, rows, wavelet, records, source_pos, receiver_pos, state, hits)

    @pl.when(d == 1)
    def _():
        surface_rows(1, 0, rows, wavelet, records, source_pos, receiver_pos, state, hits)
        w_col = as_column(surface_angular[pl.ds(1, 1), :])

        def step(l, carry):
            tables[...] = layer_tables(w_col, model, l, rows, width, 16)
            for r0 in range(0, rows, SUB):
                def emit(k, value):
                    at = pl.ds(k * LANES, LANES)
                    if r0 == 0:
                        totals[l, :, at] = value
                    else:
                        totals[l, :, at] += value
                layer_tile(state, tables, r0, rows, emit)
            return carry

        lax.fori_loop(0, 4, step, 0)
        scale = 1.0 / math.sqrt(rows)
        image = [jnp.sum(totals[l], axis=0, keepdims=True) * scale for l in range(4)]
        for l in range(4):
            total = 2.0 * image[l]
            if l > 0:
                total = total - 0.5 * image[l - 1]
            if l < 3:
                total = total - 0.5 * image[l + 1]
            sent[l : l + 1, :] = total + above[...] if l == 3 else total
        extra[...] = -0.5 * image[3]

    @pl.when(d < 2)
    def _():
        out[0] = state[...]


def close_kernel(
    first, relayed, second, top, own, from1, from2, below, extra, section, fields_out, sems,
):
    d = lax.axis_index("depth")
    rows = relayed.shape[0] // 4

    def move(source, base, start, count, slot):
        return [
            pltpu.make_async_copy(
                source.at[pl.ds(c * base, count), :],
                fields_out.at[0, c, pl.ds(start, count), :],
                sems.at[slot + c],
            )
            for c in range(4)
        ]

    def run(copies):
        for copy in copies:
            copy.start()

    local = d < 2
    is_relayed = jnp.logical_and(d % 4 == 1, d > 1)

    @pl.when(local)
    def _():
        run([pltpu.make_async_copy(top.at[0, c, pl.ds(0, rows), :], fields_out.at[0, c, pl.ds(0, rows), :], sems.at[c]) for c in range(4)])
        run([pltpu.make_async_copy(top.at[0, c, pl.ds(rows, rows), :], fields_out.at[0, c, pl.ds(rows, rows), :], sems.at[4 + c]) for c in range(4)])

    @pl.when(jnp.logical_not(local))
    def _():
        run(move(second, rows, rows, rows, 4))

        @pl.when(is_relayed)
        def _():
            run(move(relayed, rows, 0, rows, 0))

        @pl.when(jnp.logical_not(is_relayed))
        def _():
            run(move(first, rows, 0, rows, 0))

    section[...] = own[...] + from1[...] + from2[...] + below[...]
    section[0:1, :] += extra[...] + second[4 * rows : 4 * rows + 1, :]
    for copy in move(first, rows, 0, rows, 0) + move(second, rows, rows, rows, 4):
        copy.wait()


VMEM = pl.BlockSpec(memory_space=pltpu.VMEM)
SMEM = pl.BlockSpec(memory_space=pltpu.SMEM)
ANY = pl.BlockSpec(memory_space=pl.ANY)
PARAMS = pltpu.CompilerParams(vmem_limit_bytes=40 * 2**20)


def f32(*shape):
    return jax.ShapeDtypeStruct(shape, jnp.float32)


def on_device(
    devices,
    fields_in, flight_angular, wavelet, surface_angular, records, source_pos, receiver_pos, vel_table, vel_index,
):
    width = fields_in.shape[3]
    freqs = fields_in.shape[2]
    receivers = records.shape[3]
    levels = vel_table.shape[1]
    rows = freqs // 2
    axis = "depth"
    positions = receiver_pos.reshape(1, receivers)
    model = jnp.concatenate(
        [
            vel_index.astype(jnp.float32),
            jnp.pad(jnp.concatenate([vel_table] * 3, axis=1), ((0, 0), (0, width - 3 * levels))),
        ],
        axis=0,
    )
    last = devices - 1
    model1 = lax.ppermute(model, axis, [(i, (i - 1) % devices) for i in range(devices)])
    model2 = lax.ppermute(model, axis, [(i, i - 2) for i in range(2, devices)] + [(1, last)])
    model_above = lax.ppermute(model, axis, [(0, 1)])

    def main(chunk, earlier):
        last_chunk = earlier is not None
        ins = [fields_in, flight_angular, surface_angular, wavelet, records, source_pos, positions, model, model1, model2]
        specs = [
            pl.BlockSpec((1, 4, rows, width), lambda i: (0, 0, chunk, 0)),
            VMEM, VMEM, VMEM, VMEM, SMEM, VMEM, VMEM, VMEM, VMEM,
        ]
        if last_chunk:
            ins.append(earlier)
            specs.append(VMEM)
            outs = (f32(4 * rows + 8, width), f32(4, width), f32(4, width), f32(4, width), f32(1, width))
        else:
            outs = (f32(4 * rows, width), f32(4 * TICKS, width))

        def body(*refs):
            main_kernel(chunk, rows, devices, last_chunk, *refs)

        return pl.pallas_call(
            body,
            grid=(1,),
            out_shape=outs,
            in_specs=specs,
            out_specs=[VMEM] * len(outs),
            scratch_shapes=[
                pltpu.VMEM((4, rows, width), jnp.float32),
                pltpu.VMEM((3 * rows, width), jnp.float32),
                pltpu.VMEM((4 * TICKS, SUB, width), jnp.float32),
                pltpu.VMEM((24, width), jnp.float32),
                pltpu.VMEM((width, receivers), jnp.bfloat16),
            ],
            compiler_params=PARAMS,
            name="blocks",
        )(*ins)

    on = [(i, i + 3) for i in range(devices - 3)]
    direct = on + [(last, 2)]
    via = [(i, i - 1) if i % 4 == 2 else (i, j) for i, j in on] + [(last, 2)]
    relay = [(i, i + 4) for i in range(1, devices - 4, 4)]

    sent1, partial = main(0, None)
    first = lax.ppermute(sent1, axis, via)
    sent2, own, next1, next2, above = main(1, partial)
    second = lax.ppermute(sent2, axis, direct)
    relayed = lax.ppermute(first, axis, relay)
    from1 = lax.ppermute(next1, axis, [(i, (i + 1) % devices) for i in range(devices)])
    from2 = lax.ppermute(next2, axis, [(i, i + 2) for i in range(devices - 2)] + [(last, 1)])
    sent_up, extra, top = pl.pallas_call(
        top_kernel,
        out_shape=(f32(4, width), f32(1, width), f32(1, 4, freqs, width)),
        in_specs=[VMEM, VMEM, VMEM, VMEM, SMEM, VMEM, VMEM],
        out_specs=[VMEM] * 3,
        scratch_shapes=[
            pltpu.VMEM((4, freqs, width), jnp.float32),
            pltpu.VMEM((3 * freqs, width), jnp.float32),
            pltpu.VMEM((4, SUB, width), jnp.float32),
            pltpu.VMEM((width, receivers), jnp.bfloat16),
        ],
        compiler_params=PARAMS,
        name="top",
    )(above, surface_angular, wavelet, records, source_pos, positions, model_above)
    below = lax.ppermute(sent_up, axis, [(i, i - 1) for i in range(1, devices)])
    section, fields_out = pl.pallas_call(
        close_kernel,
        out_shape=(f32(4, width), f32(1, 4, freqs, width)),
        in_specs=[ANY, ANY, VMEM, ANY, VMEM, VMEM, VMEM, VMEM, VMEM],
        out_specs=[VMEM, ANY],
        scratch_shapes=[pltpu.SemaphoreType.DMA((8,))],
        compiler_params=PARAMS,
        name="close",
    )(first, relayed, second, top, own, from1, from2, below, extra)
    return section, fields_out


def solution(mesh):
    placed = (
        P("depth", None, "shots", None),
        P("depth", "shots"),
        P(None, None, "shots"),
        P(None, "shots"),
        P(None, None, "shots", None),
        P("shots"),
        P("shots"),
        P("depth", None),
        P("depth", None),
    )
    devices = mesh.shape["depth"]

    def run(*args):
        return on_device(devices, *args)

    return jax.shard_map(
        run,
        mesh=mesh,
        in_specs=placed,
        out_specs=(P("depth", "shots"), P("depth", None, "shots", None)),
        check_vma=False,
    )
```

```python
import math

import jax
import jax.numpy as jnp
from jax import lax
from jax.experimental import pallas as pl
from jax.experimental.pallas import tpu as pltpu
from jax.sharding import PartitionSpec as P

TICKS = 3
SUB = 8
LANES = 128
LAYERS = 4

depth_step = 1.0
lateral_scale = 0.03
damping = 0.3


COS = (0.9999999956, -0.4999999227, 0.04166644492, -0.001388656022, 2.469073179e-05, -2.510758575e-07)
SINC = (0.9999999997, -0.1666666607, 0.00833331612, -0.0001983946321, 2.747139839e-06, -2.315705927e-08)


def horner(coefficients, z):
    total = jnp.full(z.shape, coefficients[-1], jnp.float32)
    for c in coefficients[-2::-1]:
        total = total * z + c
    return total


def iota(shape, axis):
    return lax.broadcasted_iota(jnp.int32, shape, axis)


def as_column(row):
    n = row.shape[1]
    return jnp.sum(jnp.where(iota((n, n), 0) == iota((n, n), 1), row, 0.0), axis=1, keepdims=True)


def repeated(column):
    n = column.shape[0]
    return jnp.sum(jnp.where(iota((n, LANES), 0) == iota((n, LANES), 1) % n, column, 0.0), axis=0, keepdims=True)


def pieces_of(value, count):
    found = []
    for i in range(count):
        piece = value.astype(jnp.bfloat16)
        found.append(piece)
        if i + 1 < count:
            value = value - piece.astype(jnp.float32)
    return found


class Shape:
    def __init__(self, rows, width):
        self.rows, self.width = rows, width
        self.parts = LANES // rows
        self.cells = width // self.parts
        self.steps = self.cells // SUB


def load_field(shape, natural, c, flat, state):
    for b in range(shape.cells // LANES):
        stacked = jnp.concatenate(
            [natural(q * shape.cells + b * LANES) for q in range(shape.parts)], axis=0
        )
        flat[b * LANES : (b + 1) * LANES, :] = stacked.T
    for k in range(shape.steps):
        state[c, k * SUB : (k + 1) * SUB, :] = flat[pl.ds(k, SUB, stride=shape.steps), :]


def turned_back(shape, ref, b):
    rows = []
    for x in range(b * LANES, (b + 1) * LANES, SUB):
        sub, k = x // shape.steps, x % shape.steps
        rows.append(ref[pl.ds(k * SUB + sub, SUB, stride=SUB), :])
    return jnp.concatenate(rows, axis=0).T


def store_field(shape, c, state, put):
    for b in range(shape.cells // LANES):
        turned = turned_back(shape, state.at[c], b)
        for q in range(shape.parts):
            put(q * shape.cells + b * LANES, turned[q * shape.rows : (q + 1) * shape.rows, :])


def load_slowness(shape, models, flat, slowness):
    count = LAYERS * shape.parts
    for b in range(shape.cells // LANES):
        rows = [m[:, b * LANES : (b + 1) * LANES] for m in models]
        rows.append(jnp.zeros((LANES - len(models) * count, LANES), jnp.float32))
        flat[b * LANES : (b + 1) * LANES, :] = jnp.concatenate(rows, axis=0).T
    for k in range(0, shape.steps, 2):
        pair = jnp.concatenate([flat[pl.ds(k + i, SUB, stride=shape.steps), :] for i in range(2)], axis=0)
        for i, piece in enumerate(pieces_of(pair, 3)):
            slowness[k * SUB : (k + 2) * SUB, i * LANES : (i + 1) * LANES] = piece


def layer_slowness(shape, l, slowness, spread):
    chosen = jnp.where(
        iota((LANES, LANES), 0) == l * shape.parts + iota((LANES, LANES), 1) // shape.rows, 1.0, 0.0
    ).astype(jnp.bfloat16)
    spread[...] = jnp.dot(slowness[...], jnp.concatenate([chosen] * 3, axis=0), preferred_element_type=jnp.float32)


def layer_step(shape, state, w_row, spread, products):
    n = shape.steps
    sub, lane = iota((SUB, LANES), 0), iota((SUB, LANES), 1)
    rows = shape.rows
    cell, gains = {}, {}
    gain = lateral_scale * depth_step / 24.0

    def below(v):
        r = pltpu.roll(v, 1, 0)
        return jnp.where(sub == 0, jnp.where(lane < rows, 0.0, pltpu.roll(r, rows, 1)), r)

    def above(v):
        r = pltpu.roll(v, SUB - 1, 0)
        return jnp.where(sub == SUB - 1, jnp.where(lane >= LANES - rows, 0.0, pltpu.roll(r, LANES - rows, 1)), r)

    def turn(k):
        at = pl.ds(k * SUB, SUB)
        sr, si, rr, ri = (state[c, at, :] for c in range(4))
        phase = w_row * spread[at, :]
        square = phase * phase
        cosine = horner(COS, square)
        sine = horner(SINC, square) * phase
        rough = pl.reciprocal(phase, approx=True)
        gains[k] = rough * (2.0 * gain - (gain * phase) * rough)
        cell[k] = [
            sr * cosine - si * sine,
            sr * sine + si * cosine,
            rr * cosine + ri * sine,
            ri * cosine - rr * sine,
        ]

    for k in (n - 2, n - 1, 0, 1):
        turn(k)
    cell[-1], cell[-2] = [below(v) for v in cell[n - 1]], [below(v) for v in cell[n - 2]]
    cell[n], cell[n + 1] = [above(v) for v in cell[0]], [above(v) for v in cell[1]]
    slope, bend = {}, {}

    def slope_of(k):
        slope[k] = [b - a for a, b in zip(cell[k], cell[k + 1])]

    def bend_of(k):
        bend[k] = [b - a for a, b in zip(slope[k - 1], slope[k])]

    for k in (-2, -1, 0):
        slope_of(k)
    for k in (-1, 0):
        bend_of(k)
    for k in range(n):
        if k + 2 not in cell:
            turn(k + 2)
        slope_of(k + 1)
        bend_of(k + 1)
        curve = [14.0 * e - (a + b) for a, e, b in zip(bend[k - 1], bend[k], bend[k + 1])]
        g = gains[k]
        new = [
            cell[k][0] + g * (damping * curve[0] - curve[1]),
            cell[k][1] + g * (damping * curve[1] + curve[0]),
            cell[k][2] + g * (damping * curve[2] + curve[3]),
            cell[k][3] + g * (damping * curve[3] - curve[2]),
        ]
        for c in range(4):
            state[c, k * SUB : (k + 1) * SUB, :] = new[c]
        products[k * SUB : (k + 1) * SUB, :] = new[0] * new[2] + new[1] * new[3]


def add_contribution(shape, l, products, totals):
    picked = jnp.where(
        iota((LANES, LANES), 1) == l * shape.parts + iota((LANES, LANES), 0) // shape.rows, 1.0, 0.0
    ).astype(jnp.bfloat16)
    pieces = jnp.concatenate(pieces_of(products[...], 2), axis=1)
    totals[...] += jnp.dot(pieces, jnp.concatenate([picked] * 2, axis=0), preferred_element_type=jnp.float32)


def image_of(shape, totals, image):
    for b in range(shape.cells // LANES):
        image[:, b * LANES : (b + 1) * LANES] = turned_back(shape, totals, b)[0 : image.shape[0], :]


def hear(t, records, receiver_pos, heard, hits, planes, sem):
    freqs, width = planes.shape[1:]
    receivers = records.shape[3]
    copy = pltpu.make_async_copy(records.at[t], heard, sem)
    copy.start()
    places = receiver_pos[...]
    for r in range(0, receivers, LANES):
        column = as_column(places[:, r : r + LANES].astype(jnp.float32)).astype(jnp.int32)
        hits[r : r + LANES, :] = jnp.where(iota((LANES, width), 1) == column, 1.0, 0.0).astype(jnp.bfloat16)
    copy.wait()
    pieces = jnp.concatenate([piece for c in range(2) for piece in pieces_of(heard[c], 3)], axis=0)
    for x in range(0, width, 512):
        found = jnp.dot(pieces, hits[:, x : x + 512], preferred_element_type=jnp.float32)
        for c in range(2):
            part = [found[(3 * c + i) * freqs : (3 * c + i + 1) * freqs] for i in range(3)]
            planes[c, :, x : x + 512] = part[0] + part[1] + part[2]


def surface_field(shape, t, f0, wavelet, source_pos, planes, flat, state):
    rows = shape.rows
    for c in range(4):
        if c < 2:
            strength = as_column(wavelet[t, c : c + 1, :])[f0 : f0 + rows]

            def natural(x, strength=strength):
                return jnp.where(iota((rows, LANES), 1) == source_pos[0] - x, strength, 0.0)
        else:
            def natural(x, c=c):
                return planes[c - 2, f0 : f0 + rows, x : x + LANES]
        load_field(shape, natural, c, flat, state)


def run_layers(shape, first, last, w_row, state, slowness, spread_a, spread_b, products, totals):
    layer_slowness(shape, 2 * first, slowness, spread_a)

    def step(i, carry):
        l = 2 * i
        layer_slowness(shape, l + 1, slowness, spread_b)
        layer_step(shape, state, w_row, spread_a, products)
        add_contribution(shape, l, products, totals)
        layer_slowness(shape, l + 2, slowness, spread_a)
        layer_step(shape, state, w_row, spread_b, products)
        add_contribution(shape, l + 1, products, totals)
        return carry

    lax.fori_loop(first, last, step, 0)


def main_kernel(
    shape, chunk, devices, last_chunk,
    fields, angular, surface_angular, wavelet, records, source_pos, receiver_pos,
    model0, model1, model2, *rest,
):
    if last_chunk:
        earlier, planes, sent, own, next1, next2, up, *scratch = rest
    else:
        sent, partial, planes, *scratch = rest
    state, spread_a, spread_b, products, totals, slowness, flat, image, heard, hits, sem = scratch
    rows, parts = shape.rows, shape.parts
    f0 = chunk * rows
    count = LAYERS * TICKS
    d = lax.axis_index("depth")
    end = d == devices - 1

    @pl.when(jnp.logical_not(end))
    def _():
        for c in range(4):
            load_field(shape, lambda x, c=c: fields[0, c, :, x : x + LANES], c, flat, state)

    @pl.when(end)
    def _():
        if not last_chunk:
            hear(0, records, receiver_pos, heard, hits, planes, sem)
        surface_field(shape, 0, f0, wavelet, source_pos, planes, flat, state)

    load_slowness(shape, (model0, model1, model2), flat, slowness)
    w_own = repeated(as_column(angular[...])[f0 : f0 + rows])
    w_top = repeated(as_column(surface_angular[0:1, :])[f0 : f0 + rows])
    w_row = jnp.broadcast_to(jnp.where(end, w_top, w_own), (SUB, LANES))
    totals[...] = jnp.zeros(totals.shape, jnp.float32)
    run_layers(shape, jnp.where(end, LAYERS // 2, 0), count // 2, w_row, state, slowness, spread_a, spread_b, products, totals)
    for c in range(4):
        def put(x, value, c=c):
            sent[c * rows : (c + 1) * rows, x : x + LANES] = value
        store_field(shape, c, state, put)
    if not last_chunk:
        image_of(shape, totals, partial)
        return
    image_of(shape, totals, image)
    scale = 1.0 / math.sqrt(angular.shape[1])
    found = []
    for l in range(count):
        at = pl.ds(l * parts, parts)
        value = (image[at, :] + earlier[at, :]) * scale
        if l >= 2 * LAYERS:
            value = jnp.where(d == devices - 2, 0.0, value)
        found.append(value)

    def filtered(l):
        total = jnp.zeros_like(found[0])
        if 0 <= l < count:
            total = 2.0 * found[l]
        if l >= 1:
            total = total - 0.5 * found[l - 1]
        if l + 1 < count:
            after = found[l + 1]
            total = total - 0.5 * (jnp.where(end, 0.0, after) if l == LAYERS - 1 else after)
        return total

    up[...] = filtered(-1)
    for t, out in enumerate((own, next1, next2)):
        for l in range(LAYERS):
            out[l * parts : (l + 1) * parts, :] = filtered(t * LAYERS + l)
    sent[4 * rows : 4 * rows + parts, 0 : shape.cells] = filtered(count)


def rest_kernel(
    shape, freqs, devices,
    up, fields, angular, surface_angular, wavelet, records, source_pos, receiver_pos, model, model_above,
    sent, extra, out,
    state, spread_a, spread_b, products, totals, slowness, flat, image, heard, hits, planes, held, sem,
):
    rows, parts = shape.rows, shape.parts
    d = lax.axis_index("depth")
    end = d == devices - 1
    top = d == 1
    sent[...] = jnp.zeros(sent.shape, jnp.float32)
    sent[(LAYERS - 1) * parts : LAYERS * parts, :] = up[...]
    extra[...] = jnp.zeros(extra.shape, jnp.float32)

    def keep(f0):
        for c in range(4):
            def put(x, value, c=c):
                out[0, c, f0 : f0 + rows, x : x + LANES] = value
            store_field(shape, c, state, put)

    @pl.when(d == 0)
    def _():
        hear(2, records, receiver_pos, heard, hits, planes, sem)
        for f0 in range(0, freqs, rows):
            surface_field(shape, 2, f0, wavelet, source_pos, planes, flat, state)
            keep(f0)

    @pl.when(jnp.logical_or(top, end))
    def _():
        @pl.when(top)
        def _():
            hear(1, records, receiver_pos, heard, hits, planes, sem)

        @pl.when(end)
        def _():
            copy = pltpu.make_async_copy(fields.at[0], held, sem)
            copy.start()
            copy.wait()

        totals[...] = jnp.zeros(totals.shape, jnp.float32)
        picked = jnp.where(top, model_above[...], model[...])
        load_slowness(shape, (picked,), flat, slowness)
        for f0 in range(0, freqs, rows):
            @pl.when(top)
            def _():
                surface_field(shape, 1, f0, wavelet, source_pos, planes, flat, state)

            @pl.when(end)
            def _():
                for c in range(4):
                    load_field(shape, lambda x, c=c: held[c, f0 : f0 + rows, x : x + LANES], c, flat, state)

            w_own = repeated(as_column(angular[...])[f0 : f0 + rows])
            w_top = repeated(as_column(surface_angular[1:2, :])[f0 : f0 + rows])
            w_row = jnp.broadcast_to(jnp.where(top, w_top, w_own), (SUB, LANES))
            run_layers(shape, 0, LAYERS // 2, w_row, state, slowness, spread_a, spread_b, products, totals)

            @pl.when(top)
            def _():
                keep(f0)
        image_of(shape, totals, image)
        scale = 1.0 / math.sqrt(freqs)
        found = [image[l * parts : (l + 1) * parts, :] * scale for l in range(LAYERS)]
        rows_of = []
        for l in range(LAYERS):
            total = 2.0 * found[l]
            if l > 0:
                total = total - 0.5 * found[l - 1]
            if l + 1 < LAYERS:
                total = total - 0.5 * found[l + 1]
            rows_of.append(total)

        @pl.when(top)
        def _():
            for l in range(LAYERS):
                sent[l * parts : (l + 1) * parts, :] = rows_of[l] + up[...] if l == LAYERS - 1 else rows_of[l]
            extra[0:parts, :] = -0.5 * found[LAYERS - 1]

        @pl.when(end)
        def _():
            for l in range(LAYERS):
                extra[l * parts : (l + 1) * parts, :] = rows_of[l]
            sent[(LAYERS - 1) * parts : LAYERS * parts, :] = -0.5 * found[0]


def slowness_kernel(table, index, out):
    layers, width = index.shape
    levels = table.shape[1]
    cells = out.shape[1]
    parts = width // cells
    number = index[...]
    speed = jnp.broadcast_to(table[:, 0:1], number.shape)
    for n in range(1, levels):
        speed = jnp.where(number == n, table[:, n : n + 1], speed)
    slow = depth_step / speed
    for l in range(layers):
        for q in range(parts):
            out[l * parts + q : l * parts + q + 1, :] = slow[l : l + 1, q * cells : (q + 1) * cells]


def close_kernel(
    first, relayed, second, tail, top, own, from1, from2, below, extra, section, fields_out, sems,
):
    d = lax.axis_index("depth")
    rows = relayed.shape[0] // 4

    def move(source, base, start, count, slot):
        return [
            pltpu.make_async_copy(
                source.at[pl.ds(c * base, count), :],
                fields_out.at[0, c, pl.ds(start, count), :],
                sems.at[slot + c],
            )
            for c in range(4)
        ]

    def run(copies):
        for copy in copies:
            copy.start()

    local = d < 2
    is_relayed = jnp.logical_and(d % 4 == 1, d > 1)

    @pl.when(local)
    def _():
        run([pltpu.make_async_copy(top.at[0, c, pl.ds(0, rows), :], fields_out.at[0, c, pl.ds(0, rows), :], sems.at[c]) for c in range(4)])
        run([pltpu.make_async_copy(top.at[0, c, pl.ds(rows, rows), :], fields_out.at[0, c, pl.ds(rows, rows), :], sems.at[4 + c]) for c in range(4)])

    @pl.when(jnp.logical_not(local))
    def _():
        run(move(second, rows, rows, rows, 4))

        @pl.when(is_relayed)
        def _():
            run(move(relayed, rows, 0, rows, 0))

        @pl.when(jnp.logical_not(is_relayed))
        def _():
            run(move(first, rows, 0, rows, 0))

    parts, cells = extra.shape[0] // LAYERS, extra.shape[1]
    total = own[...] + from1[...] + from2[...] + below[...] + extra[...]
    for l in range(LAYERS):
        rows_of = total[l * parts : (l + 1) * parts, :]
        if l == 0:
            rows_of = rows_of + tail[0:parts, 0:cells]
        for q in range(parts):
            section[l : l + 1, q * cells : (q + 1) * cells] = rows_of[q : q + 1, :]
    for copy in move(first, rows, 0, rows, 0) + move(second, rows, rows, rows, 4):
        copy.wait()


VMEM = pl.BlockSpec(memory_space=pltpu.VMEM)
SMEM = pl.BlockSpec(memory_space=pltpu.SMEM)
HBM = pl.BlockSpec(memory_space=pltpu.HBM)
ANY = pl.BlockSpec(memory_space=pl.ANY)
PARAMS = pltpu.CompilerParams(vmem_limit_bytes=40 * 2**20)


def f32(*shape):
    return jax.ShapeDtypeStruct(shape, jnp.float32)


def scratch_of(shape, receivers, freqs, count):
    square = pltpu.VMEM((SUB * shape.steps, LANES), jnp.float32)
    return [
        pltpu.VMEM((4, SUB * shape.steps, LANES), jnp.float32),
        square,
        square,
        square,
        square,
        pltpu.VMEM((SUB * shape.steps, 3 * LANES), jnp.bfloat16),
        square,
        pltpu.VMEM((count * shape.parts, shape.cells), jnp.float32),
        pltpu.VMEM((2, freqs, receivers), jnp.float32),
        pltpu.VMEM((receivers, shape.width), jnp.bfloat16),
    ]


def on_device(
    devices,
    fields_in, flight_angular, wavelet, surface_angular, records, source_pos, receiver_pos, vel_table, vel_index,
):
    width = fields_in.shape[3]
    freqs = fields_in.shape[2]
    receivers = records.shape[3]
    rows = freqs // 2
    shape = Shape(rows, width)
    parts, cells, count = shape.parts, shape.cells, LAYERS * TICKS
    axis = "depth"
    positions = receiver_pos.reshape(1, receivers)
    near = f32(LAYERS * parts, cells)
    model = pl.pallas_call(
        slowness_kernel,
        out_shape=near,
        in_specs=[VMEM, VMEM],
        out_specs=VMEM,
        compiler_params=PARAMS,
        name="slowness",
    )(vel_table, vel_index)
    last = devices - 1
    model1 = lax.ppermute(model, axis, [(i, (i - 1) % devices) for i in range(devices)])
    model2 = lax.ppermute(model, axis, [(i, (i - 2) % devices) for i in range(devices)])
    model_above = lax.ppermute(model, axis, [(0, 1)])

    def main(chunk, earlier, planes):
        last_chunk = earlier is not None
        ins = [fields_in, flight_angular, surface_angular, wavelet, records, source_pos, positions, model, model1, model2]
        specs = [
            pl.BlockSpec((1, 4, rows, width), lambda i: (0, 0, chunk, 0)),
            VMEM, VMEM, VMEM, HBM, SMEM, VMEM, VMEM, VMEM, VMEM,
        ]
        if last_chunk:
            ins += [earlier, planes]
            specs += [VMEM, VMEM]
            outs = (f32(4 * rows + SUB, width), near, near, near, f32(parts, cells))
        else:
            outs = (f32(4 * rows, width), f32(count * parts, cells), f32(2, freqs, width))

        def body(*refs):
            main_kernel(shape, chunk, devices, last_chunk, *refs)

        return pl.pallas_call(
            body,
            grid=(1,),
            out_shape=outs,
            in_specs=specs,
            out_specs=[VMEM] * len(outs),
            scratch_shapes=scratch_of(shape, receivers, freqs, count) + [pltpu.SemaphoreType.DMA],
            compiler_params=PARAMS,
            name="blocks",
        )(*ins)

    on = [(i, i + 3) for i in range(devices - 3)]
    direct = on + [(last, 2)]
    via = [(i, i - 1) if i % 4 == 2 else (i, j) for i, j in on] + [(last, 2)]
    relay = [(i, i + 4) for i in range(1, devices - 4, 4)]

    sent1, partial, planes = main(0, None, None)
    first = lax.ppermute(sent1, axis, via)
    sent2, own, next1, next2, up = main(1, partial, planes)
    second = lax.ppermute(sent2, axis, direct)
    relayed = lax.ppermute(first, axis, relay)
    from1 = lax.ppermute(next1, axis, [(i, (i + 1) % devices) for i in range(devices)])
    from2 = lax.ppermute(next2, axis, [(i, i + 2) for i in range(devices - 2)] + [(last, 1)])
    sent_up, extra, top = pl.pallas_call(
        lambda *refs: rest_kernel(shape, freqs, devices, *refs),
        out_shape=(near, near, f32(1, 4, freqs, width)),
        in_specs=[VMEM, HBM, VMEM, VMEM, VMEM, HBM, SMEM, VMEM, VMEM, VMEM],
        out_specs=[VMEM] * 3,
        scratch_shapes=scratch_of(shape, receivers, freqs, LAYERS)
        + [
            pltpu.VMEM((2, freqs, width), jnp.float32),
            pltpu.VMEM((4, freqs, width), jnp.float32),
            pltpu.SemaphoreType.DMA,
        ],
        compiler_params=PARAMS,
        name="rest",
    )(up, fields_in, flight_angular, surface_angular, wavelet, records, source_pos, positions, model, model_above)
    below = lax.ppermute(sent_up, axis, [(i, i - 1) for i in range(1, devices)])
    section, fields_out = pl.pallas_call(
        close_kernel,
        grid=(1,),
        out_shape=(f32(LAYERS, width), f32(1, 4, freqs, width)),
        in_specs=[ANY, ANY, ANY, pl.BlockSpec((SUB, width), lambda i: (4 * rows // SUB, 0)), ANY, VMEM, VMEM, VMEM, VMEM, VMEM],
        out_specs=[VMEM, ANY],
        scratch_shapes=[pltpu.SemaphoreType.DMA((8,))],
        compiler_params=PARAMS,
        name="close",
    )(first, relayed, second, second, top, own, from1, from2, below, extra)
    return section, fields_out


def solution(mesh):
    placed = (
        P("depth", None, "shots", None),
        P("depth", "shots"),
        P(None, None, "shots"),
        P(None, "shots"),
        P(None, None, "shots", None),
        P("shots"),
        P("shots"),
        P("depth", None),
        P("depth", None),
    )
    devices = mesh.shape["depth"]

    def run(*args):
        return on_device(devices, *args)

    return jax.shard_map(
        run,
        mesh=mesh,
        in_specs=placed,
        out_specs=(P("depth", "shots"), P("depth", None, "shots", None)),
        check_vma=False,
    )
```

```python
import math

import jax
import jax.numpy as jnp
from jax import lax
from jax.experimental import pallas as pl
from jax.experimental.pallas import tpu as pltpu
from jax.sharding import PartitionSpec as P

TICKS = 3
SUB = 8
LANES = 128
LAYERS = 4
LEVELS = 16

depth_step = 1.0
lateral_scale = 0.03
damping = 0.3


COS = (0.9999999956, -0.4999999227, 0.04166644492, -0.001388656022, 2.469073179e-05, -2.510758575e-07)
SINC = (0.9999999997, -0.1666666607, 0.00833331612, -0.0001983946321, 2.747139839e-06, -2.315705927e-08)


def horner(coefficients, z):
    total = jnp.full(z.shape, coefficients[-1], jnp.float32)
    for c in coefficients[-2::-1]:
        total = total * z + c
    return total


def iota(shape, axis):
    return lax.broadcasted_iota(jnp.int32, shape, axis)


def as_column(row):
    n = row.shape[1]
    return jnp.sum(jnp.where(iota((n, n), 0) == iota((n, n), 1), row, 0.0), axis=1, keepdims=True)


def repeated(column):
    n = column.shape[0]
    return jnp.sum(jnp.where(iota((n, LANES), 0) == iota((n, LANES), 1) % n, column, 0.0), axis=0, keepdims=True)


def pieces_of(value, count):
    found = []
    for i in range(count):
        piece = value.astype(jnp.bfloat16)
        found.append(piece)
        if i + 1 < count:
            value = value - piece.astype(jnp.float32)
    return found


class Shape:
    def __init__(self, rows, width):
        self.rows, self.width = rows, width
        self.parts = LANES // rows
        self.cells = width // self.parts
        self.steps = self.cells // SUB


def load_field(shape, natural, c, flat, state):
    for b in range(shape.cells // LANES):
        stacked = jnp.concatenate(
            [natural(q * shape.cells + b * LANES) for q in range(shape.parts)], axis=0
        )
        flat[b * LANES : (b + 1) * LANES, :] = stacked.T
    for k in range(shape.steps):
        state[c, k * SUB : (k + 1) * SUB, :] = flat[pl.ds(k, SUB, stride=shape.steps), :]


def turned_back(shape, ref, b):
    rows = []
    for x in range(b * LANES, (b + 1) * LANES, SUB):
        sub, k = x // shape.steps, x % shape.steps
        rows.append(ref[pl.ds(k * SUB + sub, SUB, stride=SUB), :])
    return jnp.concatenate(rows, axis=0).T


def store_field(shape, c, state, put):
    for b in range(shape.cells // LANES):
        turned = turned_back(shape, state.at[c], b)
        for q in range(shape.parts):
            put(q * shape.cells + b * LANES, turned[q * shape.rows : (q + 1) * shape.rows, :])


def load_known(shape, models, flat, known):
    parts, count = shape.parts, LAYERS * shape.parts
    for t, model in enumerate(models):
        number = model[0:count, :]
        speeds = []
        for l in range(LAYERS):
            own = number[l * parts : (l + 1) * parts, :]
            table = model[count + l : count + l + 1, 0:LEVELS]
            speed = jnp.broadcast_to(table[:, 0:1], own.shape)
            for n in range(1, LEVELS):
                speed = jnp.where(own == float(n), table[:, n : n + 1], speed)
            speeds.append(jnp.where(speed > 0.0, speed, 1.0))
        rows = [number] + [piece.astype(jnp.float32) for piece in pieces_of(jnp.concatenate(speeds, axis=0), 3)]
        stacked = jnp.concatenate(rows, axis=0)
        for b in range(shape.cells // LANES):
            flat[b * LANES : (b + 1) * LANES, :] = stacked[:, b * LANES : (b + 1) * LANES].T
        for k in range(0, shape.steps, 2):
            pair = [flat[pl.ds(k + i, SUB, stride=shape.steps), :] for i in range(2)]
            known[k * SUB : (k + 2) * SUB, t * LANES : (t + 1) * LANES] = jnp.concatenate(pair, axis=0).astype(jnp.bfloat16)


def layer_tables(shape, l, w_row, speed_row, known, weights, tables, gains):
    count = LAYERS * shape.parts
    row, lane = iota((LANES, 2 * LANES), 0), iota((LANES, 2 * LANES), 1)
    mine = row % count == l * shape.parts + lane % LANES // shape.rows
    chosen = jnp.where(jnp.logical_and(mine, (row < count) == (lane < LANES)), 1.0, 0.0).astype(jnp.bfloat16)
    spread = jnp.dot(known, chosen, preferred_element_type=jnp.float32)
    level = (iota((1, LANES), 1) % LEVELS).astype(jnp.float32)
    hot = jnp.where(spread[:, :LANES] == level, 1.0, 0.0).astype(jnp.bfloat16)
    gains[...] = spread[:, LANES:] * ((lateral_scale / 24.0) / w_row)
    phase = w_row * (depth_step / as_column(jnp.where(speed_row > 0.0, speed_row, 1.0)))
    z = phase * phase
    own = iota((LEVELS, LANES), 1) // shape.rows
    for t, table in enumerate((horner(COS, z), horner(SINC, z) * phase)):
        for i, piece in enumerate(pieces_of(table, 2)):
            piece = piece.astype(jnp.float32)
            for q in range(shape.parts):
                at = (i * shape.parts + q) * LEVELS
                weights[at : at + LEVELS, t * LANES : (t + 1) * LANES] = jnp.where(own == q, piece, 0.0).astype(jnp.bfloat16)
    tables[...] = jnp.dot(jnp.concatenate([hot, hot], axis=1), weights[...], preferred_element_type=jnp.float32)


def layer_step(shape, state, tables, gains, products):
    n = shape.steps
    sub, lane = iota((SUB, LANES), 0), iota((SUB, LANES), 1)
    rows = shape.rows
    cell = {}

    def below(v):
        r = pltpu.roll(v, 1, 0)
        return jnp.where(sub == 0, jnp.where(lane < rows, 0.0, pltpu.roll(r, rows, 1)), r)

    def above(v):
        r = pltpu.roll(v, SUB - 1, 0)
        return jnp.where(sub == SUB - 1, jnp.where(lane >= LANES - rows, 0.0, pltpu.roll(r, LANES - rows, 1)), r)

    def turn(k):
        at = pl.ds(k * SUB, SUB)
        sr, si, rr, ri = (state[c, at, :] for c in range(4))
        cosine, sine = tables[at, 0:LANES], tables[at, LANES : 2 * LANES]
        cell[k] = [
            sr * cosine - si * sine,
            sr * sine + si * cosine,
            rr * cosine + ri * sine,
            ri * cosine - rr * sine,
        ]

    for k in (n - 2, n - 1, 0, 1):
        turn(k)
    cell[-1], cell[-2] = [below(v) for v in cell[n - 1]], [below(v) for v in cell[n - 2]]
    cell[n], cell[n + 1] = [above(v) for v in cell[0]], [above(v) for v in cell[1]]
    slope, bend = {}, {}

    def slope_of(k):
        slope[k] = [b - a for a, b in zip(cell[k], cell[k + 1])]

    def bend_of(k):
        bend[k] = [b - a for a, b in zip(slope[k - 1], slope[k])]

    for k in (-2, -1, 0):
        slope_of(k)
    for k in (-1, 0):
        bend_of(k)
    for k in range(n):
        if k + 2 not in cell:
            turn(k + 2)
        slope_of(k + 1)
        bend_of(k + 1)
        curve = [14.0 * e - (a + b) for a, e, b in zip(bend[k - 1], bend[k], bend[k + 1])]
        g = gains[k * SUB : (k + 1) * SUB, :]
        new = [
            cell[k][0] + g * (damping * curve[0] - curve[1]),
            cell[k][1] + g * (damping * curve[1] + curve[0]),
            cell[k][2] + g * (damping * curve[2] + curve[3]),
            cell[k][3] + g * (damping * curve[3] - curve[2]),
        ]
        for c in range(4):
            state[c, k * SUB : (k + 1) * SUB, :] = new[c]
        products[k * SUB : (k + 1) * SUB, :] = new[0] * new[2] + new[1] * new[3]


def add_contribution(shape, l, products, totals):
    picked = jnp.where(
        iota((LANES, LANES), 1) == l * shape.parts + iota((LANES, LANES), 0) // shape.rows, 1.0, 0.0
    ).astype(jnp.bfloat16)
    pieces = jnp.concatenate(pieces_of(products[...], 2), axis=1)
    totals[...] += jnp.dot(pieces, jnp.concatenate([picked] * 2, axis=0), preferred_element_type=jnp.float32)


def image_of(shape, totals, image):
    for b in range(shape.cells // LANES):
        image[:, b * LANES : (b + 1) * LANES] = turned_back(shape, totals, b)[0 : image.shape[0], :]


def hear(t, records, receiver_pos, heard, hits, planes, sem):
    freqs, width = planes.shape[1:]
    receivers = records.shape[3]
    copy = pltpu.make_async_copy(records.at[t], heard, sem)
    copy.start()
    places = receiver_pos[...]
    for r in range(0, receivers, LANES):
        column = as_column(places[:, r : r + LANES].astype(jnp.float32)).astype(jnp.int32)
        hits[r : r + LANES, :] = jnp.where(iota((LANES, width), 1) == column, 1.0, 0.0).astype(jnp.bfloat16)
    copy.wait()
    pieces = jnp.concatenate([piece for c in range(2) for piece in pieces_of(heard[c], 3)], axis=0)
    for x in range(0, width, 512):
        found = jnp.dot(pieces, hits[:, x : x + 512], preferred_element_type=jnp.float32)
        for c in range(2):
            part = [found[(3 * c + i) * freqs : (3 * c + i + 1) * freqs] for i in range(3)]
            planes[c, :, x : x + 512] = part[0] + part[1] + part[2]


def surface_field(shape, t, f0, wavelet, source_pos, planes, flat, state):
    rows = shape.rows
    for c in range(4):
        if c < 2:
            strength = as_column(wavelet[t, c : c + 1, :])[f0 : f0 + rows]

            def natural(x, strength=strength):
                return jnp.where(iota((rows, LANES), 1) == source_pos[0] - x, strength, 0.0)
        else:
            def natural(x, c=c):
                return planes[c - 2, f0 : f0 + rows, x : x + LANES]
        load_field(shape, natural, c, flat, state)


class Work:
    def __init__(self, refs):
        self.state, self.totals, self.flat, self.known = refs[:4]
        self.products, self.weights, self.tables, self.gains = refs[4:6], refs[6:8], refs[8:10], refs[10:12]


def work_scratch(shape, models):
    cells = SUB * shape.steps
    square = pltpu.VMEM((cells, LANES), jnp.float32)
    return [
        pltpu.VMEM((4, cells, LANES), jnp.float32),
        square,
        square,
        pltpu.VMEM((cells, models * LANES), jnp.bfloat16),
        square,
        square,
        pltpu.VMEM((2 * LANES, 2 * LANES), jnp.bfloat16),
        pltpu.VMEM((2 * LANES, 2 * LANES), jnp.bfloat16),
        pltpu.VMEM((cells, 2 * LANES), jnp.float32),
        pltpu.VMEM((cells, 2 * LANES), jnp.float32),
        square,
        square,
    ]


def run_layers(shape, work, w_row, models, first=0, contribute=True):
    count = LAYERS * len(models)

    def look(i):
        t, l = i // LAYERS, i % LAYERS
        at = LAYERS * shape.parts + l
        known = work.known[:, (first + t) * LANES : (first + t + 1) * LANES]
        layer_tables(
            shape, l, w_row, models[t][at : at + 1, 0:LEVELS], known,
            work.weights[i % 2], work.tables[i % 2], work.gains[i % 2],
        )

    look(0)
    for i in range(count):
        if i + 1 < count:
            look(i + 1)
        layer_step(shape, work.state, work.tables[i % 2], work.gains[i % 2], work.products[i % 2])
        if contribute:
            add_contribution(shape, first * LAYERS + i, work.products[i % 2], work.totals)


def w_row_of(angular, f0, rows):
    return repeated(as_column(angular)[f0 : f0 + rows])


def start_all(copies):
    for copy in copies:
        copy.start()


def wait_all(copies):
    for copy in copies:
        copy.wait()


def begin_kernel(
    shape,
    table, index, records, receiver_pos, wavelet, source_pos,
    model, planes, top,
    own_table, own_index, places, heard, hits, found, own_wavelet, kept, sems,
):
    parts, cells = shape.parts, shape.cells
    copies = [
        pltpu.make_async_copy(table, own_table, sems.at[0]),
        pltpu.make_async_copy(index, own_index, sems.at[1]),
    ]
    start_all(copies)
    wait_all(copies)
    number = own_index[...].astype(jnp.float32)
    for l in range(LAYERS):
        for q in range(parts):
            model[l * parts + q : l * parts + q + 1, :] = number[l : l + 1, q * cells : (q + 1) * cells]
    model[LAYERS * parts : LAYERS * parts + LAYERS, 0:LEVELS] = own_table[...]
    d = lax.axis_index("depth")

    @pl.when(d < 2)
    def _():
        copies = [
            pltpu.make_async_copy(receiver_pos, places, sems.at[0]),
            pltpu.make_async_copy(wavelet, own_wavelet, sems.at[1]),
        ]
        start_all(copies)
        wait_all(copies)
        hear(jnp.where(d == 0, TICKS - 1, TICKS - 2), records, places, heard, hits, found, sems.at[0])

    @pl.when(d == 0)
    def _():
        for c in range(2):
            strength = as_column(own_wavelet[TICKS - 1, c : c + 1, :])
            kept[c] = jnp.where(iota(kept.shape[1:], 1) == source_pos[0], strength, 0.0)
            kept[2 + c] = found[c]
        copy = pltpu.make_async_copy(kept, top, sems.at[0])
        copy.start()
        copy.wait()

    @pl.when(d == 1)
    def _():
        copy = pltpu.make_async_copy(found, planes, sems.at[0])
        copy.start()
        copy.wait()


def own_layers(shape, chunks, fields, angular, model, held, own_angular, sems, work, each):
    rows = shape.rows
    angles = pltpu.make_async_copy(angular, own_angular, sems.at[chunks])
    copies = [pltpu.make_async_copy(fields.at[0, :, pl.ds(i * rows, rows), :], held.at[i], sems.at[i]) for i in range(chunks)]
    start_all([angles] + copies)
    load_known(shape, (model,), work.flat, work.known)
    work.totals[...] = jnp.zeros(work.totals.shape, jnp.float32)
    angles.wait()
    for i in range(chunks):
        copies[i].wait()
        for c in range(4):
            load_field(shape, lambda x, c=c: held[i, c, :, x : x + LANES], c, work.flat, work.state)
        w_row = w_row_of(own_angular[...], i * rows, rows)
        run_layers(shape, work, w_row, (model,))
        each(i, w_row)


def first_kernel(
    shape, chunks, devices,
    fields, angular, model, surface_angular, records, receiver_pos, wavelet, source_pos,
    after, image, w_rows,
    held, own_angular, own_surface, own_wavelet, places, heard, hits, found, sems, *scratch,
):
    work = Work(scratch)
    rows = shape.rows
    d = lax.axis_index("depth")

    def keep(i, w_row):
        after[i] = work.state[...]
        w_rows[i * SUB : (i + 1) * SUB, :] = jnp.broadcast_to(w_row, (SUB, LANES))

    @pl.when(d < devices - 1)
    def _():
        own_layers(shape, chunks, fields, angular, model, held, own_angular, sems, work, keep)
        image_of(shape, work.totals, image)

    @pl.when(d == devices - 1)
    def _():
        copies = [
            pltpu.make_async_copy(receiver_pos, places, sems.at[0]),
            pltpu.make_async_copy(surface_angular, own_surface, sems.at[1]),
            pltpu.make_async_copy(wavelet, own_wavelet, sems.at[2]),
        ]
        start_all(copies)
        wait_all(copies)
        hear(0, records, places, heard, hits, found, sems.at[0])
        for i in range(chunks):
            surface_field(shape, 0, i * rows, own_wavelet, source_pos, found, work.flat, work.state)
            keep(i, w_row_of(own_surface[0:1, :], i * rows, rows))
        image[...] = jnp.zeros(image.shape, jnp.float32)


def rows_at(ref, l, parts):
    return ref[l * parts : (l + 1) * parts, :]


def next_kernel(shape, freqs, devices, chunk, *refs):
    rows, parts = shape.rows, shape.parts
    after, w_rows, mate, two, mate_two, *refs = refs
    d = lax.axis_index("depth")
    if chunk:
        before, next_a, sent, own, next1, next2, up, shared, image, *scratch = refs
    else:
        sent, image, *scratch = refs
    work = Work(scratch)
    work.state[...] = after[chunk]
    models = (jnp.where(d % 2 == 0, mate[...], mate_two[...]), two)
    load_known(shape, models, work.flat, work.known)
    work.totals[...] = jnp.zeros(work.totals.shape, jnp.float32)
    run_layers(shape, work, w_rows[chunk * SUB : chunk * SUB + 1, :], models)
    for c in range(4):
        def put(x, value, c=c):
            sent[c * rows : (c + 1) * rows, x : x + LANES] = value
        store_field(shape, c, work.state, put)
    image_of(shape, work.totals, image)
    if not chunk:
        return
    scale = 1.0 / math.sqrt(freqs)
    count = LAYERS * TICKS
    found = []
    for l in range(count):
        if l < LAYERS:
            value = rows_at(before, l, parts) * scale
        else:
            value = (rows_at(image, l - LAYERS, parts) + rows_at(next_a, l - LAYERS, parts)) * scale
        if l >= 2 * LAYERS:
            value = jnp.where(d == devices - 2, 0.0, value)
        found.append(value)

    def beside(l, other):
        lower = max(l, other)
        return found[other] if lower % LAYERS else jnp.where(d == devices - lower // LAYERS, 0.0, found[other])

    def filtered(l):
        total = 2.0 * found[l]
        if l > 0:
            total = total - 0.5 * beside(l, l - 1)
        if l + 1 < count:
            total = total - 0.5 * beside(l, l + 1)
        return total

    up[...] = -0.5 * found[0]
    for t, out in enumerate((own, next1, next2)):
        for l in range(LAYERS):
            out[l * parts : (l + 1) * parts, :] = filtered(t * LAYERS + l)
    sent[4 * rows : 4 * rows + parts, 0 : shape.cells] = -0.5 * found[count - 1]
    near = LAYERS * parts
    even = d % 2 == 0
    shared[0:near, :] = jnp.where(even, next1[...], 0.0)
    shared[near : 2 * near, :] = jnp.where(even, next2[...], 0.0)

    @pl.when(jnp.logical_not(even))
    def _():
        shared[near - parts : near, :] = up[...]


def late_kernel(
    shape, chunks, devices,
    fields, angular, surface_angular, wavelet, source_pos, planes, model, mate, _,
    out, shared, extra,
    held, part, kept, image, own_angular, own_surface, own_wavelet, sems, *scratch,
):
    work = Work(scratch)
    rows, parts = shape.rows, shape.parts
    d = lax.axis_index("depth")
    shared[...] = jnp.zeros(shared.shape, jnp.float32)
    extra[...] = jnp.zeros(extra.shape, jnp.float32)

    def filtered():
        image_of(shape, work.totals, image)
        scale = 1.0 / math.sqrt(chunks * rows)
        found = [rows_at(image, l, parts) * scale for l in range(LAYERS)]
        totals = []
        for l in range(LAYERS):
            total = 2.0 * found[l]
            if l > 0:
                total = total - 0.5 * found[l - 1]
            if l + 1 < LAYERS:
                total = total - 0.5 * found[l + 1]
            totals.append(total)
        return found, totals

    @pl.when(d == 1)
    def _():
        copies = [
            pltpu.make_async_copy(planes, part, sems.at[0]),
            pltpu.make_async_copy(surface_angular, own_surface, sems.at[1]),
            pltpu.make_async_copy(wavelet, own_wavelet, sems.at[2]),
        ]
        start_all(copies)
        load_known(shape, (mate,), work.flat, work.known)
        work.totals[...] = jnp.zeros(work.totals.shape, jnp.float32)
        wait_all(copies)
        for i in range(chunks):
            surface_field(shape, 1, i * rows, own_wavelet, source_pos, part, work.flat, work.state)
            run_layers(shape, work, w_row_of(own_surface[1:2, :], i * rows, rows), (mate,))
            for c in range(4):
                def put(x, value, c=c):
                    kept[c, i * rows : (i + 1) * rows, x : x + LANES] = value
                store_field(shape, c, work.state, put)
        copy = pltpu.make_async_copy(kept, out, sems.at[0])
        copy.start()
        found, totals = filtered()
        for l in range(LAYERS):
            shared[l * parts : (l + 1) * parts, :] = totals[l]
        extra[0:parts, :] = -0.5 * found[LAYERS - 1]
        copy.wait()

    @pl.when(d == devices - 1)
    def _():
        own_layers(shape, chunks, fields, angular, model, held, own_angular, sems, work, lambda i, w_row: None)
        found, totals = filtered()
        for l in range(LAYERS):
            extra[l * parts : (l + 1) * parts, :] = totals[l]
        shared[(LAYERS - 1) * parts : LAYERS * parts, :] = -0.5 * found[0]


def mix_kernel(next1, next2, up, other, out):
    near, parts = next1.shape[0], up.shape[0]
    even = lax.axis_index("depth") % 2 == 0
    out[0:near, :] = jnp.where(even, 0.0, other[near : 2 * near, :] + next1[...])
    out[near : 2 * near, :] = jnp.where(even, 0.0, next2[...])

    @pl.when(even)
    def _():
        out[near - parts : near, :] = up[...]


def pass_kernel(crossed, late, out):
    near = late.shape[0]
    out[...] = jnp.where(lax.axis_index("depth") % 2 == 0, crossed[near : 2 * near, :], late[...])


def close_kernel(first, relayed, second, top, top1, own, other, crossed, passed, extra, section, fields_out, sems):
    near, cells = own.shape
    parts = near // LAYERS
    rows = relayed.shape[0] // 4
    d = lax.axis_index("depth")

    def moves(source, start, slot):
        return [
            pltpu.make_async_copy(
                source.at[pl.ds(c * rows, rows), :], fields_out.at[0, c, pl.ds(start, rows), :], sems.at[slot + c]
            )
            for c in range(4)
        ]

    for index, field in enumerate((top, top1)):
        @pl.when(d == index)
        def _(field=field):
            for c in range(4):
                for i in range(2):
                    at = pl.ds(i * rows, rows)
                    pltpu.make_async_copy(field.at[c, at, :], fields_out.at[0, c, at, :], sems.at[4 * i + c]).start()

    @pl.when(d > 1)
    def _():
        start_all(moves(second, rows, 4))

        @pl.when(d % 4 == 1)
        def _():
            start_all(moves(relayed, 0, 0))

        @pl.when(d % 4 != 1)
        def _():
            start_all(moves(first, 0, 0))

    total = own[...] + other[0:near, :] + crossed[0:near, :] + passed[...] + extra[...]
    for l in range(LAYERS):
        rows_of = total[l * parts : (l + 1) * parts, :]
        if l == 0:
            rows_of = rows_of + second[4 * rows : 4 * rows + parts, 0:cells]
        for q in range(parts):
            section[l : l + 1, q * cells : (q + 1) * cells] = rows_of[q : q + 1, :]
    wait_all(moves(first, 0, 0) + moves(second, rows, 4))


VMEM = pl.BlockSpec(memory_space=pltpu.VMEM)
SMEM = pl.BlockSpec(memory_space=pltpu.SMEM)
HBM = pl.BlockSpec(memory_space=pltpu.HBM)
ANY = pl.BlockSpec(memory_space=pl.ANY)
COST = pl.CostEstimate(flops=0, bytes_accessed=0, transcendentals=0)
PARAMS = pltpu.CompilerParams(vmem_limit_bytes=48 * 2**20)


def f32(*shape):
    return jax.ShapeDtypeStruct(shape, jnp.float32)


def on_device(
    devices,
    fields_in, flight_angular, wavelet, surface_angular, records, source_pos, receiver_pos, vel_table, vel_index,
):
    width = fields_in.shape[3]
    freqs = fields_in.shape[2]
    receivers = records.shape[3]
    rows = freqs // 2
    shape = Shape(rows, width)
    parts, cells = shape.parts, shape.cells
    axis = "depth"
    near, row = f32(LAYERS * parts, cells), f32(parts, cells)
    model_rows = LAYERS * parts + SUB
    chunk = f32(4 * rows + SUB, width)
    state = f32(4, SUB * shape.steps, LANES)
    planes_shape = f32(2, freqs, width)
    planes_scratch = pltpu.VMEM((2, freqs, width), jnp.float32)

    def image_scratch(ticks):
        return pltpu.VMEM((ticks * LAYERS * parts, cells), jnp.float32)

    def call(body, outs, ins, scratch, name):
        return pl.pallas_call(
            body,
            out_shape=[shape for shape, _ in outs],
            in_specs=[spec for _, spec in ins],
            out_specs=[spec for _, spec in outs],
            scratch_shapes=scratch,
            compiler_params=PARAMS,
            cost_estimate=COST,
            name=name,
        )(*[value if spec is not HBM else pltpu.with_memory_space_constraint(value, pltpu.HBM) for value, spec in ins])

    def swapped(value):
        return lax.ppermute(value, axis, [(i, i + 1 - 2 * (i % 2)) for i in range(devices)])

    chunks = 2
    last = devices - 1
    positions = receiver_pos.reshape(1, receivers)
    row_of = lambda value: pltpu.VMEM(value.shape, value.dtype)
    hearing = [
        row_of(positions), pltpu.VMEM((2, freqs, receivers), jnp.float32), pltpu.VMEM((receivers, width), jnp.bfloat16),
        planes_scratch,
    ]
    model, planes1, top = call(
        lambda *refs: begin_kernel(shape, *refs),
        [(f32(model_rows, cells), VMEM), (planes_shape, ANY), (f32(4, freqs, width), ANY)],
        [(vel_table, HBM), (vel_index, HBM), (records, HBM), (positions, HBM), (wavelet, HBM), (source_pos, SMEM)],
        [row_of(vel_table), row_of(vel_index)]
        + hearing
        + [row_of(wavelet), pltpu.VMEM((4, freqs, width), jnp.float32), pltpu.SemaphoreType.DMA((2,))],
        "begin",
    )
    mate = swapped(model)
    two = lax.ppermute(lax.optimization_barrier((model, mate))[0], axis, [(i, (i - 2) % devices) for i in range(devices)])
    held = pltpu.VMEM((chunks, 4, rows, width), jnp.float32)
    sems = pltpu.SemaphoreType.DMA((chunks + 1,))
    after, before, w_rows = call(
        lambda *refs: first_kernel(shape, chunks, devices, *refs),
        [
            (f32(chunks, 4, SUB * shape.steps, LANES), VMEM), (near, VMEM), (f32(chunks * SUB, LANES), VMEM),
        ],
        [
            (fields_in, HBM), (flight_angular, HBM), (model, VMEM), (surface_angular, HBM), (records, HBM), (positions, HBM),
            (wavelet, HBM), (source_pos, SMEM),
        ],
        [held, row_of(flight_angular), row_of(surface_angular), row_of(wavelet)] + hearing + [sems] + work_scratch(shape, 1),
        "first",
    )
    mate_two = swapped(lax.optimization_barrier((two, w_rows))[0])
    on = [(i, i + 3) for i in range(devices - 3)] + [(last, 2)]
    via = [(i, i - 1) if i % 4 == 2 else (i, j) for i, j in on]
    relay = [(i, i + 4) for i in range(1, devices - 4, 4)]
    common = [
        (after, VMEM), (w_rows, VMEM), (mate, VMEM), (two, VMEM), (mate_two, VMEM),
    ]
    again = work_scratch(shape, 2)
    both = f32(2 * LAYERS * parts, cells)
    sent1, next_a = call(
        lambda *refs: next_kernel(shape, freqs, devices, 0, *refs),
        [(f32(4 * rows, width), VMEM), (f32(2 * LAYERS * parts, cells), VMEM)],
        common,
        again,
        "next",
    )
    first = lax.ppermute(sent1, axis, via)
    sent2, own, next1, next2, up, shared = call(
        lambda *refs: next_kernel(shape, freqs, devices, 1, *refs),
        [(chunk, VMEM), (near, VMEM), (near, VMEM), (near, VMEM), (row, VMEM), (both, VMEM)],
        common + [(before, VMEM), (next_a, VMEM)],
        [image_scratch(2)] + again,
        "next",
    )
    second = lax.ppermute(sent2, axis, on)
    other = swapped(shared)
    (mixed,) = call(mix_kernel, [(both, VMEM)], [(next1, VMEM), (next2, VMEM), (up, VMEM), (other, VMEM)], [], "mix")
    crossed = lax.ppermute(
        mixed, axis, [(i, (i + 1) % devices) for i in range(1, devices, 2)] + [(i, i - 1) for i in range(2, devices, 2)]
    )
    relayed = lax.ppermute(lax.optimization_barrier((first, mixed))[0], axis, relay)
    top1, late, extra = call(
        lambda *refs: late_kernel(shape, chunks, devices, *refs),
        [(f32(4, freqs, width), ANY), (near, VMEM), (near, VMEM)],
        [
            (fields_in, HBM), (flight_angular, HBM), (surface_angular, HBM), (wavelet, HBM), (source_pos, SMEM),
            (planes1, ANY), (model, VMEM), (mate, VMEM), (mixed, VMEM),
        ],
        [
            held, planes_scratch, pltpu.VMEM((4, freqs, width), jnp.float32), image_scratch(1),
            row_of(flight_angular), row_of(surface_angular), row_of(wavelet), sems,
        ]
        + work_scratch(shape, 1),
        "late",
    )
    (passing,) = call(pass_kernel, [(near, VMEM)], [(crossed, VMEM), (late, VMEM)], [], "pass")
    passed = swapped(passing)
    section, fields_out = call(
        close_kernel,
        [(f32(LAYERS, width), VMEM), (f32(1, 4, freqs, width), ANY)],
        [
            (first, VMEM), (relayed, VMEM), (second, VMEM), (top, ANY), (top1, ANY),
            (own, VMEM), (other, VMEM), (crossed, VMEM), (passed, VMEM), (extra, VMEM),
        ],
        [pltpu.SemaphoreType.DMA((8,))],
        "close",
    )
    return section, fields_out


def solution(mesh):
    placed = (
        P("depth", None, "shots", None),
        P("depth", "shots"),
        P(None, None, "shots"),
        P(None, "shots"),
        P(None, None, "shots", None),
        P("shots"),
        P("shots"),
        P("depth", None),
        P("depth", None),
    )
    devices = mesh.shape["depth"]

    def run(*args):
        return on_device(devices, *args)

    return jax.shard_map(
        run,
        mesh=mesh,
        in_specs=placed,
        out_specs=(P("depth", "shots"), P("depth", None, "shots", None)),
        check_vma=False,
    )
```

```python
import math

import jax
import jax.numpy as jnp
from jax import lax
from jax.experimental import pallas as pl
from jax.experimental.pallas import tpu as pltpu
from jax.sharding import PartitionSpec as P

TICKS = 3
SUB = 8
LANES = 128
LAYERS = 4
LEVELS = 16

depth_step = 1.0
lateral_scale = 0.03
damping = 0.3


COS = (0.9999999956, -0.4999999227, 0.04166644492, -0.001388656022, 2.469073179e-05, -2.510758575e-07)
SINC = (0.9999999997, -0.1666666607, 0.00833331612, -0.0001983946321, 2.747139839e-06, -2.315705927e-08)


def horner(coefficients, z):
    total = jnp.full(z.shape, coefficients[-1], jnp.float32)
    for c in coefficients[-2::-1]:
        total = total * z + c
    return total


def iota(shape, axis):
    return lax.broadcasted_iota(jnp.int32, shape, axis)


def as_column(row):
    n = row.shape[1]
    return jnp.sum(jnp.where(iota((n, n), 0) == iota((n, n), 1), row, 0.0), axis=1, keepdims=True)


def repeated(column):
    n = column.shape[0]
    return jnp.sum(jnp.where(iota((n, LANES), 0) == iota((n, LANES), 1) % n, column, 0.0), axis=0, keepdims=True)


def pieces_of(value, count):
    found = []
    for i in range(count):
        piece = value.astype(jnp.bfloat16)
        found.append(piece)
        if i + 1 < count:
            value = value - piece.astype(jnp.float32)
    return found


class Shape:
    def __init__(self, rows, width):
        self.rows, self.width = rows, width
        self.parts = LANES // rows
        self.cells = width // self.parts
        self.steps = self.cells // SUB


def load_field(shape, natural, c, flat, state):
    for b in range(shape.cells // LANES):
        stacked = jnp.concatenate(
            [natural(q * shape.cells + b * LANES) for q in range(shape.parts)], axis=0
        )
        flat[b * LANES : (b + 1) * LANES, :] = stacked.T
    for k in range(shape.steps):
        state[c, k * SUB : (k + 1) * SUB, :] = flat[pl.ds(k, SUB, stride=shape.steps), :]


def turned_back(shape, ref, b):
    rows = []
    for x in range(b * LANES, (b + 1) * LANES, SUB):
        sub, k = x // shape.steps, x % shape.steps
        rows.append(ref[pl.ds(k * SUB + sub, SUB, stride=SUB), :])
    return jnp.concatenate(rows, axis=0).T


def store_field(shape, c, state, put):
    for b in range(shape.cells // LANES):
        turned = turned_back(shape, state.at[c], b)
        for q in range(shape.parts):
            put(q * shape.cells + b * LANES, turned[q * shape.rows : (q + 1) * shape.rows, :])


def load_known(shape, models, flat, known):
    parts, count = shape.parts, LAYERS * shape.parts
    for t, model in enumerate(models):
        number = model[0:count, :]
        speeds = []
        for l in range(LAYERS):
            own = number[l * parts : (l + 1) * parts, :]
            table = model[count + l : count + l + 1, 0:LEVELS]
            speed = jnp.broadcast_to(table[:, 0:1], own.shape)
            for n in range(1, LEVELS):
                speed = jnp.where(own == float(n), table[:, n : n + 1], speed)
            speeds.append(jnp.where(speed > 0.0, speed, 1.0))
        rows = [number] + [piece.astype(jnp.float32) for piece in pieces_of(jnp.concatenate(speeds, axis=0), 3)]
        stacked = jnp.concatenate(rows, axis=0)
        for b in range(shape.cells // LANES):
            flat[b * LANES : (b + 1) * LANES, :] = stacked[:, b * LANES : (b + 1) * LANES].T
        for k in range(0, shape.steps, 2):
            pair = [flat[pl.ds(k + i, SUB, stride=shape.steps), :] for i in range(2)]
            known[k * SUB : (k + 2) * SUB, t * LANES : (t + 1) * LANES] = jnp.concatenate(pair, axis=0).astype(jnp.bfloat16)


def layer_tables(shape, l, w_row, speed_row, known, weights, tables, gains):
    count = LAYERS * shape.parts
    row, lane = iota((LANES, 2 * LANES), 0), iota((LANES, 2 * LANES), 1)
    mine = row % count == l * shape.parts + lane % LANES // shape.rows
    chosen = jnp.where(jnp.logical_and(mine, (row < count) == (lane < LANES)), 1.0, 0.0).astype(jnp.bfloat16)
    spread = jnp.dot(known, chosen, preferred_element_type=jnp.float32)
    level = (iota((1, LANES), 1) % LEVELS).astype(jnp.float32)
    hot = jnp.where(spread[:, :LANES] == level, 1.0, 0.0).astype(jnp.bfloat16)
    gains[...] = spread[:, LANES:] * ((lateral_scale / 24.0) / w_row)
    phase = w_row * (depth_step / as_column(jnp.where(speed_row > 0.0, speed_row, 1.0)))
    z = phase * phase
    own = iota((LEVELS, LANES), 1) // shape.rows
    for t, table in enumerate((horner(COS, z), horner(SINC, z) * phase)):
        for i, piece in enumerate(pieces_of(table, 2)):
            piece = piece.astype(jnp.float32)
            for q in range(shape.parts):
                at = (i * shape.parts + q) * LEVELS
                weights[at : at + LEVELS, t * LANES : (t + 1) * LANES] = jnp.where(own == q, piece, 0.0).astype(jnp.bfloat16)
    tables[...] = jnp.dot(jnp.concatenate([hot, hot], axis=1), weights[...], preferred_element_type=jnp.float32)


def layer_step(shape, state, tables, gains, products):
    n = shape.steps
    sub, lane = iota((SUB, LANES), 0), iota((SUB, LANES), 1)
    rows = shape.rows
    cell = {}

    def below(v):
        r = pltpu.roll(v, 1, 0)
        return jnp.where(sub == 0, jnp.where(lane < rows, 0.0, pltpu.roll(r, rows, 1)), r)

    def above(v):
        r = pltpu.roll(v, SUB - 1, 0)
        return jnp.where(sub == SUB - 1, jnp.where(lane >= LANES - rows, 0.0, pltpu.roll(r, LANES - rows, 1)), r)

    def turn(k):
        at = pl.ds(k * SUB, SUB)
        sr, si, rr, ri = (state[c, at, :] for c in range(4))
        cosine, sine = tables[at, 0:LANES], tables[at, LANES : 2 * LANES]
        cell[k] = [
            sr * cosine - si * sine,
            sr * sine + si * cosine,
            rr * cosine + ri * sine,
            ri * cosine - rr * sine,
        ]

    for k in (n - 2, n - 1, 0, 1):
        turn(k)
    cell[-1], cell[-2] = [below(v) for v in cell[n - 1]], [below(v) for v in cell[n - 2]]
    cell[n], cell[n + 1] = [above(v) for v in cell[0]], [above(v) for v in cell[1]]
    slope, bend = {}, {}

    def slope_of(k):
        slope[k] = [b - a for a, b in zip(cell[k], cell[k + 1])]

    def bend_of(k):
        bend[k] = [b - a for a, b in zip(slope[k - 1], slope[k])]

    for k in (-2, -1, 0):
        slope_of(k)
    for k in (-1, 0):
        bend_of(k)
    for k in range(n):
        if k + 2 not in cell:
            turn(k + 2)
        slope_of(k + 1)
        bend_of(k + 1)
        curve = [14.0 * e - (a + b) for a, e, b in zip(bend[k - 1], bend[k], bend[k + 1])]
        g = gains[k * SUB : (k + 1) * SUB, :]
        new = [
            cell[k][0] + g * (damping * curve[0] - curve[1]),
            cell[k][1] + g * (damping * curve[1] + curve[0]),
            cell[k][2] + g * (damping * curve[2] + curve[3]),
            cell[k][3] + g * (damping * curve[3] - curve[2]),
        ]
        for c in range(4):
            state[c, k * SUB : (k + 1) * SUB, :] = new[c]
        products[k * SUB : (k + 1) * SUB, :] = new[0] * new[2] + new[1] * new[3]


def add_contribution(shape, l, products, totals):
    picked = jnp.where(
        iota((LANES, LANES), 1) == l * shape.parts + iota((LANES, LANES), 0) // shape.rows, 1.0, 0.0
    ).astype(jnp.bfloat16)
    pieces = jnp.concatenate(pieces_of(products[...], 2), axis=1)
    totals[...] += jnp.dot(pieces, jnp.concatenate([picked] * 2, axis=0), preferred_element_type=jnp.float32)


def image_of(shape, totals, image):
    for b in range(shape.cells // LANES):
        image[:, b * LANES : (b + 1) * LANES] = turned_back(shape, totals, b)[0 : image.shape[0], :]


def hear(t, records, receiver_pos, heard, hits, planes, sem):
    freqs, width = planes.shape[1:]
    receivers = records.shape[3]
    copy = pltpu.make_async_copy(records.at[t], heard, sem)
    copy.start()
    places = receiver_pos[...]
    for r in range(0, receivers, LANES):
        column = as_column(places[:, r : r + LANES].astype(jnp.float32)).astype(jnp.int32)
        hits[r : r + LANES, :] = jnp.where(iota((LANES, width), 1) == column, 1.0, 0.0).astype(jnp.bfloat16)
    copy.wait()
    pieces = jnp.concatenate([piece for c in range(2) for piece in pieces_of(heard[c], 3)], axis=0)
    for x in range(0, width, 512):
        found = jnp.dot(pieces, hits[:, x : x + 512], preferred_element_type=jnp.float32)
        for c in range(2):
            part = [found[(3 * c + i) * freqs : (3 * c + i + 1) * freqs] for i in range(3)]
            planes[c, :, x : x + 512] = part[0] + part[1] + part[2]


def surface_field(shape, t, f0, wavelet, source_pos, planes, flat, state):
    rows = shape.rows
    for c in range(4):
        if c < 2:
            strength = as_column(wavelet[t, c : c + 1, :])[f0 : f0 + rows]

            def natural(x, strength=strength):
                return jnp.where(iota((rows, LANES), 1) == source_pos[0] - x, strength, 0.0)
        else:
            def natural(x, c=c):
                return planes[c - 2, f0 : f0 + rows, x : x + LANES]
        load_field(shape, natural, c, flat, state)


class Work:
    def __init__(self, refs):
        self.state, self.totals, self.flat, self.known = refs[:4]
        self.products, self.weights, self.tables, self.gains = refs[4:6], refs[6:8], refs[8:10], refs[10:12]


def work_scratch(shape, models):
    cells = SUB * shape.steps
    square = pltpu.VMEM((cells, LANES), jnp.float32)
    return [
        pltpu.VMEM((4, cells, LANES), jnp.float32),
        square,
        square,
        pltpu.VMEM((cells, models * LANES), jnp.bfloat16),
        square,
        square,
        pltpu.VMEM((2 * LANES, 2 * LANES), jnp.bfloat16),
        pltpu.VMEM((2 * LANES, 2 * LANES), jnp.bfloat16),
        pltpu.VMEM((cells, 2 * LANES), jnp.float32),
        pltpu.VMEM((cells, 2 * LANES), jnp.float32),
        square,
        square,
    ]


def run_layers(shape, work, w_row, models, first=0, contribute=True):
    count = LAYERS * len(models)

    def look(i):
        t, l = i // LAYERS, i % LAYERS
        at = LAYERS * shape.parts + l
        known = work.known[:, (first + t) * LANES : (first + t + 1) * LANES]
        layer_tables(
            shape, l, w_row, models[t][at : at + 1, 0:LEVELS], known,
            work.weights[i % 2], work.tables[i % 2], work.gains[i % 2],
        )

    look(0)
    for i in range(count):
        if i + 1 < count:
            look(i + 1)
        layer_step(shape, work.state, work.tables[i % 2], work.gains[i % 2], work.products[i % 2])
        if contribute:
            add_contribution(shape, first * LAYERS + i, work.products[i % 2], work.totals)


def w_row_of(angular, f0, rows):
    return repeated(as_column(angular)[f0 : f0 + rows])


def start_all(copies):
    for copy in copies:
        copy.start()


def wait_all(copies):
    for copy in copies:
        copy.wait()


def begin_kernel(
    shape,
    table, index, records, receiver_pos, wavelet, source_pos,
    model, planes, top,
    own_table, own_index, places, heard, hits, found, own_wavelet, kept, sems,
):
    parts, cells = shape.parts, shape.cells
    copies = [
        pltpu.make_async_copy(table, own_table, sems.at[0]),
        pltpu.make_async_copy(index, own_index, sems.at[1]),
    ]
    start_all(copies)
    wait_all(copies)
    number = own_index[...].astype(jnp.float32)
    for l in range(LAYERS):
        for q in range(parts):
            model[l * parts + q : l * parts + q + 1, :] = number[l : l + 1, q * cells : (q + 1) * cells]
    model[LAYERS * parts : LAYERS * parts + LAYERS, 0:LEVELS] = own_table[...]
    d = lax.axis_index("depth")

    @pl.when(d < 2)
    def _():
        copies = [
            pltpu.make_async_copy(receiver_pos, places, sems.at[0]),
            pltpu.make_async_copy(wavelet, own_wavelet, sems.at[1]),
        ]
        start_all(copies)
        wait_all(copies)
        hear(jnp.where(d == 0, TICKS - 1, TICKS - 2), records, places, heard, hits, found, sems.at[0])

    @pl.when(d == 0)
    def _():
        for c in range(2):
            strength = as_column(own_wavelet[TICKS - 1, c : c + 1, :])
            kept[c] = jnp.where(iota(kept.shape[1:], 1) == source_pos[0], strength, 0.0)
            kept[2 + c] = found[c]
        copy = pltpu.make_async_copy(kept, top, sems.at[0])
        copy.start()
        copy.wait()

        hear(1, records, places, heard, hits, found, sems.at[0])

    @pl.when(d < 2)
    def _():
        copy = pltpu.make_async_copy(found, planes, sems.at[0])
        copy.start()
        copy.wait()


def own_layers(shape, which, fields, angular, model, held, own_angular, sems, work, each):
    rows = shape.rows
    angles = pltpu.make_async_copy(angular, own_angular, sems.at[sems.shape[0] - 1])
    copies = {i: pltpu.make_async_copy(fields.at[0, :, pl.ds(i * rows, rows), :], held.at[i], sems.at[i]) for i in which}
    start_all([angles] + list(copies.values()))
    load_known(shape, (model,), work.flat, work.known)
    work.totals[...] = jnp.zeros(work.totals.shape, jnp.float32)
    angles.wait()
    for i in which:
        copies[i].wait()
        for c in range(4):
            load_field(shape, lambda x, c=c: held[i, c, :, x : x + LANES], c, work.flat, work.state)
        w_row = w_row_of(own_angular[...], i * rows, rows)
        run_layers(shape, work, w_row, (model,))
        each(i, w_row)


def first_kernel(
    shape, chunks, devices,
    fields, angular, model, surface_angular, records, receiver_pos, wavelet, source_pos,
    after, image, w_rows, early,
    held, own_angular, own_surface, own_wavelet, places, heard, hits, found, sems, *scratch,
):
    work = Work(scratch)
    rows = shape.rows
    d = lax.axis_index("depth")

    def keep(i, w_row):
        after[i] = work.state[...]
        w_rows[i * SUB : (i + 1) * SUB, :] = jnp.broadcast_to(w_row, (SUB, LANES))

    @pl.when(d < devices - 1)
    def _():
        own_layers(shape, range(chunks), fields, angular, model, held, own_angular, sems, work, keep)
        image_of(shape, work.totals, image)

    @pl.when(d == devices - 1)
    def _():
        copies = [
            pltpu.make_async_copy(receiver_pos, places, sems.at[0]),
            pltpu.make_async_copy(surface_angular, own_surface, sems.at[1]),
            pltpu.make_async_copy(wavelet, own_wavelet, sems.at[2]),
        ]
        start_all(copies)
        wait_all(copies)
        hear(0, records, places, heard, hits, found, sems.at[0])
        for i in range(chunks):
            surface_field(shape, 0, i * rows, own_wavelet, source_pos, found, work.flat, work.state)
            keep(i, w_row_of(own_surface[0:1, :], i * rows, rows))
        image[...] = jnp.zeros(image.shape, jnp.float32)
        own_layers(shape, range(1), fields, angular, model, held, own_angular, sems, work, lambda i, w_row: None)
        image_of(shape, work.totals, early)


def rows_at(ref, l, parts):
    return ref[l * parts : (l + 1) * parts, :]


def next_kernel(shape, freqs, devices, chunk, *refs):
    rows, parts = shape.rows, shape.parts
    after, w_rows, mate, two, mate_two, *refs = refs
    d = lax.axis_index("depth")
    if chunk:
        before, next_a, sent, own, shared, across, next2, image, *scratch = refs
    else:
        sent, image, *scratch = refs
    work = Work(scratch)
    work.state[...] = after[chunk]
    models = (jnp.where(d % 2 == 0, mate[...], mate_two[...]), two)
    load_known(shape, models, work.flat, work.known)
    work.totals[...] = jnp.zeros(work.totals.shape, jnp.float32)
    run_layers(shape, work, w_rows[chunk * SUB : chunk * SUB + 1, :], models)
    for c in range(4):
        def put(x, value, c=c):
            sent[c * rows : (c + 1) * rows, x : x + LANES] = value
        store_field(shape, c, work.state, put)
    image_of(shape, work.totals, image)
    if not chunk:
        return
    scale = 1.0 / math.sqrt(freqs)
    count = LAYERS * TICKS
    found = []
    for l in range(count):
        if l < LAYERS:
            value = rows_at(before, l, parts) * scale
        else:
            value = (rows_at(image, l - LAYERS, parts) + rows_at(next_a, l - LAYERS, parts)) * scale
        if l >= 2 * LAYERS:
            value = jnp.where(d == devices - 2, 0.0, value)
        found.append(value)

    def beside(l, other):
        lower = max(l, other)
        return found[other] if lower % LAYERS else jnp.where(d == devices - lower // LAYERS, 0.0, found[other])

    def filtered(l):
        total = 2.0 * found[l]
        if l > 0:
            total = total - 0.5 * beside(l, l - 1)
        if l + 1 < count:
            total = total - 0.5 * beside(l, l + 1)
        return total

    even = d % 2 == 0
    for l in range(LAYERS):
        at = pl.ds(l * parts, parts)
        own[at, :] = filtered(l)
        below = filtered(LAYERS + l)
        above = -0.5 * found[0] if l == LAYERS - 1 else jnp.zeros_like(below)
        shared[at, :] = jnp.where(even, below, above)
        across[at, :] = jnp.where(even, above, below)
        next2[at, :] = filtered(2 * LAYERS + l)
    sent[4 * rows : 4 * rows + parts, 0 : shape.cells] = -0.5 * found[count - 1]


def late_kernel(
    shape, chunks, devices,
    fields, angular, surface_angular, wavelet, source_pos, planes, model, mate, early, _,
    out, out_more, shared, extra,
    held, part, image, own_angular, own_surface, own_wavelet, sems, *scratch,
):
    work = Work(scratch)
    rows, parts = shape.rows, shape.parts
    d = lax.axis_index("depth")
    shared[...] = jnp.zeros(shared.shape, jnp.float32)
    extra[...] = jnp.zeros(extra.shape, jnp.float32)

    def filtered(more=None):
        image_of(shape, work.totals, image)
        scale = 1.0 / math.sqrt(chunks * rows)
        found = [rows_at(image, l, parts) * scale for l in range(LAYERS)]
        if more is not None:
            found = [value + rows_at(more, l, parts) * scale for l, value in enumerate(found)]
        totals = []
        for l in range(LAYERS):
            total = 2.0 * found[l]
            if l > 0:
                total = total - 0.5 * found[l - 1]
            if l + 1 < LAYERS:
                total = total - 0.5 * found[l + 1]
            totals.append(total)
        return found, totals

    @pl.when(d < 2)
    def _():
        copies = [
            pltpu.make_async_copy(planes, part, sems.at[0]),
            pltpu.make_async_copy(surface_angular, own_surface, sems.at[1]),
            pltpu.make_async_copy(wavelet, own_wavelet, sems.at[2]),
        ]
        start_all(copies)
        top_model = jnp.where(d == 0, model[...], mate[...])
        load_known(shape, (top_model,), work.flat, work.known)
        work.totals[...] = jnp.zeros(work.totals.shape, jnp.float32)
        wait_all(copies)
        for i in range(chunks):
            @pl.when(d == 1 - i)
            def _(i=i):
                surface_field(shape, 1, i * rows, own_wavelet, source_pos, part, work.flat, work.state)
        w_both = [w_row_of(own_surface[1:2, :], i * rows, rows) for i in range(chunks)]
        run_layers(shape, work, jnp.where(d == 1, w_both[0], w_both[1]), (top_model,))
        for c in range(4):
            def put(x, value, c=c):
                out[c * rows : (c + 1) * rows, x : x + LANES] = value
                out_more[c * rows : (c + 1) * rows, x : x + LANES] = value
            store_field(shape, c, work.state, put)
        found, totals = filtered()

        @pl.when(d == 1)
        def _():
            for l in range(LAYERS):
                shared[l * parts : (l + 1) * parts, :] = totals[l]
            extra[0:parts, :] = -0.5 * found[LAYERS - 1]

        @pl.when(d == 0)
        def _():
            for l in range(LAYERS):
                extra[l * parts : (l + 1) * parts, :] = totals[l]
            shared[0:parts, :] = -0.5 * found[LAYERS - 1]

    @pl.when(d == devices - 1)
    def _():
        own_layers(shape, range(1, chunks), fields, angular, model, held, own_angular, sems, work, lambda i, w_row: None)
        found, totals = filtered(early)
        for l in range(LAYERS):
            extra[l * parts : (l + 1) * parts, :] = totals[l]
        shared[(LAYERS - 1) * parts : LAYERS * parts, :] = -0.5 * found[0]


def started(copies):
    for copy in copies:
        copy.start()
    return copies


def place_kernel(first, relayed, top, top1, more, fields_out, sems):
    d = lax.axis_index("depth")
    rows = first.shape[0] // 4

    def moves(source, start=0):
        return [
            pltpu.make_async_copy(
                source.at[pl.ds(c * rows, rows), :], fields_out.at[0, c, pl.ds(start, rows), :], sems.at[c + (4 if start else 0)]
            )
            for c in range(4)
        ]

    @pl.when(d == 0)
    def _():
        wait_all(started([pltpu.make_async_copy(top, fields_out.at[0], sems.at[0])]))

    @pl.when(d == 1)
    def _():
        wait_all(started(moves(top1) + moves(more, rows)))

    @pl.when(jnp.logical_and(d > 1, d % 4 == 1))
    def _():
        wait_all(started(moves(relayed)))

    @pl.when(jnp.logical_and(d > 1, d % 4 != 1))
    def _():
        wait_all(started(moves(first)))


def close_kernel(placed, second, own, other, crossed, from2, late, extra, section, fields_out, sems):
    near, cells = own.shape
    parts = near // LAYERS
    rows = (second.shape[0] - parts) // 4
    d = lax.axis_index("depth")

    def moves():
        return [
            pltpu.make_async_copy(second.at[pl.ds(c * rows, rows), :], fields_out.at[0, c, pl.ds(rows, rows), :], sems.at[c])
            for c in range(4)
        ]

    @pl.when(d > 1)
    def _():
        started(moves())

    total = own[...] + other[...] + crossed[...] + from2[...] + late[...] + extra[...]
    for l in range(LAYERS):
        rows_of = total[l * parts : (l + 1) * parts, :]
        if l == 0:
            rows_of = rows_of + second[4 * rows : 4 * rows + parts, 0:cells]
        for q in range(parts):
            section[l : l + 1, q * cells : (q + 1) * cells] = rows_of[q : q + 1, :]

    @pl.when(d > 1)
    def _():
        wait_all(moves())


VMEM = pl.BlockSpec(memory_space=pltpu.VMEM)
SMEM = pl.BlockSpec(memory_space=pltpu.SMEM)
HBM = pl.BlockSpec(memory_space=pltpu.HBM)
ANY = pl.BlockSpec(memory_space=pl.ANY)
COST = pl.CostEstimate(flops=0, bytes_accessed=0, transcendentals=0)
PARAMS = pltpu.CompilerParams(vmem_limit_bytes=48 * 2**20)


def f32(*shape):
    return jax.ShapeDtypeStruct(shape, jnp.float32)


def on_device(
    devices,
    fields_in, flight_angular, wavelet, surface_angular, records, source_pos, receiver_pos, vel_table, vel_index,
):
    width = fields_in.shape[3]
    freqs = fields_in.shape[2]
    receivers = records.shape[3]
    rows = freqs // 2
    shape = Shape(rows, width)
    parts, cells = shape.parts, shape.cells
    axis = "depth"
    near, row = f32(LAYERS * parts, cells), f32(parts, cells)
    model_rows = LAYERS * parts + SUB
    chunk = f32(4 * rows + SUB, width)
    state = f32(4, SUB * shape.steps, LANES)
    planes_shape = f32(2, freqs, width)
    planes_scratch = pltpu.VMEM((2, freqs, width), jnp.float32)

    def image_scratch(ticks):
        return pltpu.VMEM((ticks * LAYERS * parts, cells), jnp.float32)

    def call(body, outs, ins, scratch, name, aliases={}):
        return pl.pallas_call(
            body,
            out_shape=[shape for shape, _ in outs],
            in_specs=[spec for _, spec in ins],
            out_specs=[spec for _, spec in outs],
            scratch_shapes=scratch,
            input_output_aliases=aliases,
            compiler_params=PARAMS,
            cost_estimate=COST,
            name=name,
        )(*[value if spec is not HBM else pltpu.with_memory_space_constraint(value, pltpu.HBM) for value, spec in ins])

    def swapped(value):
        return lax.ppermute(value, axis, [(i, i + 1 - 2 * (i % 2)) for i in range(devices)])

    chunks = 2
    last = devices - 1
    positions = receiver_pos.reshape(1, receivers)
    row_of = lambda value: pltpu.VMEM(value.shape, value.dtype)
    hearing = [
        row_of(positions), pltpu.VMEM((2, freqs, receivers), jnp.float32), pltpu.VMEM((receivers, width), jnp.bfloat16),
        planes_scratch,
    ]
    model, planes1, top = call(
        lambda *refs: begin_kernel(shape, *refs),
        [(f32(model_rows, cells), VMEM), (planes_shape, ANY), (f32(4, freqs, width), ANY)],
        [(vel_table, HBM), (vel_index, HBM), (records, HBM), (positions, HBM), (wavelet, HBM), (source_pos, SMEM)],
        [row_of(vel_table), row_of(vel_index)]
        + hearing
        + [row_of(wavelet), pltpu.VMEM((4, freqs, width), jnp.float32), pltpu.SemaphoreType.DMA((2,))],
        "begin",
    )
    mate = swapped(model)
    two = lax.ppermute(lax.optimization_barrier((model, mate))[0], axis, [(i, (i - 2) % devices) for i in range(devices)])
    held = pltpu.VMEM((chunks, 4, rows, width), jnp.float32)
    sems = pltpu.SemaphoreType.DMA((chunks + 1,))
    after, before, w_rows, early = call(
        lambda *refs: first_kernel(shape, chunks, devices, *refs),
        [
            (f32(chunks, 4, SUB * shape.steps, LANES), VMEM), (near, VMEM), (f32(chunks * SUB, LANES), VMEM),
            (near, VMEM),
        ],
        [
            (fields_in, HBM), (flight_angular, HBM), (model, VMEM), (surface_angular, HBM), (records, HBM), (positions, HBM),
            (wavelet, HBM), (source_pos, SMEM),
        ],
        [held, row_of(flight_angular), row_of(surface_angular), row_of(wavelet)] + hearing + [sems] + work_scratch(shape, 1),
        "first",
    )
    mate_two = swapped(lax.optimization_barrier((two, w_rows))[0])
    on = [(i, i + 3) for i in range(devices - 3)] + [(last, 2)]
    via = [(i, i - 1) if i % 4 == 2 else (i, j) for i, j in on]
    relay = [(i, i + 4) for i in range(1, devices - 4, 4)]
    common = [
        (after, VMEM), (w_rows, VMEM), (mate, VMEM), (two, VMEM), (mate_two, VMEM),
    ]
    again = work_scratch(shape, 2)
    sent1, next_a = call(
        lambda *refs: next_kernel(shape, freqs, devices, 0, *refs),
        [(f32(4 * rows, width), VMEM), (f32(2 * LAYERS * parts, cells), VMEM)],
        common,
        again,
        "next",
    )
    first = lax.ppermute(sent1, axis, via)
    sent2, own, shared, across, next2 = call(
        lambda *refs: next_kernel(shape, freqs, devices, 1, *refs),
        [(chunk, VMEM)] + [(near, VMEM)] * 4,
        common + [(before, VMEM), (next_a, VMEM)],
        [image_scratch(2)] + again,
        "next",
    )
    second = lax.ppermute(sent2, axis, on)
    other = swapped(shared)
    crossed = lax.ppermute(
        across, axis, [(i, (i + 1) % devices) for i in range(1, devices, 2)] + [(i, i - 1) for i in range(2, devices, 2)]
    )
    from2 = lax.ppermute(next2, axis, [(i, i + 2) for i in range(devices - 2)] + [(last, 1)])
    relayed = lax.ppermute(first, axis, relay)
    half_shape = f32(4 * rows, width)
    top1, more, late, extra = call(
        lambda *refs: late_kernel(shape, chunks, devices, *refs),
        [(half_shape, VMEM), (half_shape, VMEM), (near, VMEM), (near, VMEM)],
        [
            (fields_in, HBM), (flight_angular, HBM), (surface_angular, HBM), (wavelet, HBM), (source_pos, SMEM),
            (planes1, ANY), (model, VMEM), (mate, VMEM), (early, VMEM), (own, VMEM),
        ],
        [
            held, planes_scratch, image_scratch(1),
            row_of(flight_angular), row_of(surface_angular), row_of(wavelet), sems,
        ]
        + work_scratch(shape, 1),
        "late",
    )
    late = swapped(late)
    more = lax.ppermute(more, axis, [(0, 1)])
    (placed,) = call(
        place_kernel,
        [(f32(1, 4, freqs, width), ANY)],
        [(first, VMEM), (relayed, VMEM), (top, ANY), (top1, VMEM), (more, VMEM)],
        [pltpu.SemaphoreType.DMA((8,))],
        "place",
    )
    section, fields_out = call(
        close_kernel,
        [(f32(LAYERS, width), VMEM), (f32(1, 4, freqs, width), ANY)],
        [
            (placed, ANY), (second, VMEM), (own, VMEM), (other, VMEM), (crossed, VMEM), (from2, VMEM), (late, VMEM),
            (extra, VMEM),
        ],
        [pltpu.SemaphoreType.DMA((4,))],
        "close",
        {0: 1},
    )
    return section, fields_out


def solution(mesh):
    placed = (
        P("depth", None, "shots", None),
        P("depth", "shots"),
        P(None, None, "shots"),
        P(None, "shots"),
        P(None, None, "shots", None),
        P("shots"),
        P("shots"),
        P("depth", None),
        P("depth", None),
    )
    devices = mesh.shape["depth"]

    def run(*args):
        return on_device(devices, *args)

    return jax.shard_map(
        run,
        mesh=mesh,
        in_specs=placed,
        out_specs=(P("depth", "shots"), P("depth", None, "shots", None)),
        check_vma=False,
    )
```
